256 devices in a mesh: dp: 4 (over z_hi), comp: 64 (over x, y, z_lo, core).
Axes of the slice: x: 4, y: 4, z: 8 (z_hi: 4, z_lo: 2; z = z_hi * 2 + z_lo), core: 2. Of those that a mesh axis runs over, the one named last changes fastest.
Arguments:
- embeddings: bfloat16 [16384, 1024], P(('dp', 'comp')), may hold values from -6 to 6
- keep: int32 [16384], P(('dp', 'comp')), may hold values from 0 to 1
- means: float32 [8192, 1024], P('comp'), may hold values from -0.6 to 0.6
- variances: float32 [8192, 1024], P('comp'), may hold values from 0.8 to 1.25
- log_weights: float32 [8192], P('comp'), may hold values from -4 to 4
Outputs:
- new_means: float32 [8192, 1024], P('comp')
- new_vars: float32 [8192, 1024], P('comp')
- new_log_weights: float32 [8192], P('comp')
- log_lik: float32 [16384], P(('dp', 'comp'))
The draws below stay inside these ranges and needn't reach their ends.
All inputs are finite; a program needn't handle non-finite values.
Results may differ from the reference program's by a relative error of at most 0.0039.
The reference program's roundings to bfloat16 on the way (of `feats`, `coef` and `resp`) count: a program that leaves them out, or rounds other values in their place, can miss the bound.
Values may be sent and summed in bfloat16 or wider, within the bound.
No kernel may reach another device: no remote copies, remote signals or barrier semaphores. Data moves between devices by JAX's collectives and lax.ppermute only.
A program may use at most 64 MiB of HBM per device.

```python
import math
import jax
import jax.numpy as jnp
from jax import lax

D = 1024
K_DEV = 128
K = 8192
N = 16384
N_COMP = 64


def draw_keep(key, part):
    key = jax.random.fold_in(key, 7)
    index = jnp.arange(N, dtype=jnp.int32)
    ticket = jax.random.randint(key, (N,), 0, 4 * N, dtype=jnp.int32)
    return (ticket < N + index * 28 // 10).astype(jnp.int32)


def level_of(key, extent, split, least, high):
    gain = 1.0
    for position, parts in split:
        heights = jax.random.uniform(jax.random.fold_in(jax.random.fold_in(key, 6), position), (parts,), jnp.float32, least / len(split), high / len(split))
        gain = gain * jnp.repeat(jnp.exp(heights), extent[position] // parts).reshape((-1,) + (1,) * (len(extent) - 1 - position))
    return gain


def normal_values(own_key, dims, width, most, shards=(), held_as=jnp.bfloat16):
    entries = jax.random.normal(own_key, dims, jnp.float32) * width
    if len(shards) > 0:
        entries = level_of(own_key, dims, shards, -0.22, 0.18) * entries
    return jnp.clip(entries, min=-most, max=most).astype(held_as)


def setup_inputs(seed: int = 0) -> dict:
    seeds = jax.random.split(jax.random.key(seed), 6)
    embeddings = normal_values(seeds[0], (N, D), 1.0, 6.0, ((0, 256),))
    keep = draw_keep(jax.random.fold_in(seeds[5], 71), 0)
    means = normal_values(seeds[2], (K, D), 0.1, 0.6, ((0, 64),), jnp.float32)
    variances = jnp.clip(jnp.exp(math.log(1.25) - 0.4462871 * jax.random.uniform(seeds[3], (K, D), jnp.float32) ** level_of(seeds[3], (K, D), ((0, 64),), -0.2, 0.2)), 0.8, 1.25)
    log_weights = normal_values(seeds[4], (K,), 1.0, 4.0, ((0, 64),), jnp.float32)
    return {"embeddings": embeddings, "keep": keep, "means": means, "variances": variances, "log_weights": log_weights}


def features(rows):
    wide = rows.astype(jnp.float32)
    return jnp.concatenate([(wide * wide).astype(jnp.bfloat16), rows], axis=1)


def reference(embeddings, keep, means, variances, log_weights):
    feats = features(embeddings)
    prec = 1.0 / variances
    coef = jnp.concatenate([-0.5 * prec, means * prec], axis=1).astype(jnp.bfloat16)
    offset = log_weights - 0.5 * jnp.sum(means * means * prec + jnp.log(variances), axis=1) - 0.5 * D * math.log(2.0 * math.pi)
    coef_blocks = coef.reshape(N_COMP, K_DEV, 2 * D)
    offset_blocks = offset.reshape(N_COMP, K_DEV)

    def lse_step(carry, block):
        top, total = carry
        weights_mat, bias = block
        scores = jnp.dot(feats, weights_mat.T, preferred_element_type=jnp.float32) + bias
        newtop = jnp.maximum(top, jnp.max(scores, axis=1))
        total = total * jnp.exp(top - newtop) + jnp.sum(jnp.exp(scores - newtop[:, None]), axis=1)
        return (newtop, total), None

    start = (jnp.full((N,), -jnp.inf, jnp.float32), jnp.zeros((N,), jnp.float32))
    (top, total), _ = lax.scan(lse_step, start, (coef_blocks, offset_blocks))
    lse = top + jnp.log(total)
    wide_rows = embeddings.astype(jnp.float32)
    log_lik = lse + 0.5 * jnp.sum(wide_rows * wide_rows, axis=1) + 0.5 * D * math.log(2.0 * math.pi)
    keep_f = keep.astype(jnp.float32)

    def moment_step(carry, block):
        weights_mat, bias = block
        scores = jnp.dot(feats, weights_mat.T, preferred_element_type=jnp.float32) + bias
        resp = (jnp.exp(scores - lse[:, None]) * keep_f[:, None]).astype(jnp.bfloat16)
        moments = jnp.dot(resp.T, feats, preferred_element_type=jnp.float32)
        counts = jnp.sum(resp.astype(jnp.float32), axis=0)
        return carry, (moments, counts)

    _, (moments, counts) = lax.scan(moment_step, jnp.zeros((), jnp.float32), (coef_blocks, offset_blocks))
    moments = moments.reshape(K, 2 * D)
    counts = counts.reshape(K)
    kept = jnp.sum(keep_f)
    second = moments[:, :D]
    first = moments[:, D:]
    denom = counts[:, None] + 1.0
    new_means = first / denom
    new_vars = (second - 2.0 * new_means * first + new_means * new_means * counts[:, None] + 1.0) / denom
    new_log_weights = jnp.log((counts + 1.0) / (kept + K))
    return new_means, new_vars, new_log_weights, log_lik
```

```python
import functools
import math

import jax
import jax.numpy as jnp
from jax import lax
from jax.experimental import pallas as pl
from jax.experimental.pallas import tpu as pltpu
from jax.sharding import Mesh, PartitionSpec as P

F32 = jnp.float32
BF16 = jnp.bfloat16
EXT = 128
VMEM = pl.BlockSpec(memory_space=pltpu.VMEM)
SMEM = pl.BlockSpec(memory_space=pltpu.SMEM)
NT = (((1,), (1,)), ((), ()))
INTERPRET = False


def call(kernel, out_shape, n_in, flops=0, nbytes=0, smem=(), **kw):
    many = isinstance(out_shape, (list, tuple))
    n_out = len(out_shape) if many else 1
    specs = dict(
        in_specs=[SMEM if i in smem else VMEM for i in range(n_in)],
        out_specs=[VMEM] * n_out if many else VMEM,
    )
    specs.update(kw)
    return pl.pallas_call(
        kernel,
        out_shape=out_shape,
        compiler_params=pltpu.CompilerParams(vmem_limit_bytes=40 * 2**20),
        cost_estimate=pl.CostEstimate(flops=flops, bytes_accessed=nbytes, transcendentals=0),
        interpret=INTERPRET,
        **specs,
    )


def sds(shape, dtype):
    return jax.ShapeDtypeStruct(shape, dtype)


def parts(col, n):
    out = []
    for _ in range(n):
        top = col.astype(BF16).astype(F32)
        out.append(top)
        col = col - top
    return out


def lanes(cols, rows):
    lane = lax.broadcasted_iota(jnp.int32, (rows, EXT), 1)
    ext = jnp.zeros((rows, EXT), F32)
    for i, col in enumerate(cols):
        ext = jnp.where(lane == i, col, ext)
    return ext


def split_ext(ext):
    counts = ext[:, 0:1] + ext[:, 1:2]
    kept = ext[:, 2:3] + ext[:, 3:4]
    return lanes(parts(counts, 2) + parts(kept, 2), ext.shape[0]).astype(BF16)


def coef_kernel(m_ref, v_ref, w_ref, out_ref):
    rows, width = m_ref.shape
    m, v = m_ref[...], v_ref[...]
    prec = 1.0 / v
    out_ref[:, :width] = (-0.5 * prec).astype(BF16)
    out_ref[:, width : 2 * width] = (m * prec).astype(BF16)
    offset = (
        w_ref[...]
        - 0.5 * jnp.sum(m * m * prec + jnp.log(v), axis=1, keepdims=True)
        - 0.5 * width * math.log(2.0 * math.pi)
    )
    out_ref[:, 2 * width :] = lanes(parts(offset, 3), rows).astype(BF16)


def square(rows):
    wide = rows.astype(F32)
    return (wide * wide).astype(BF16)


def score_tile(e_ref, coef_ref, s_ref):
    width = e_ref.shape[1]
    rows = e_ref[...]
    s = lax.dot_general(coef_ref[:, :width], square(rows), NT, preferred_element_type=F32)
    s = s + lax.dot_general(coef_ref[:, width : 2 * width], rows, NT, preferred_element_type=F32)
    s = s + jnp.sum(coef_ref[:, 2 * width :].astype(F32), axis=1, keepdims=True)
    s_ref[...] = s
    top = jnp.max(s, axis=0, keepdims=True)
    lse = top + jnp.log(jnp.sum(jnp.exp(s - top), axis=0, keepdims=True))
    return [lse[:, i * 128 : (i + 1) * 128] for i in range(lse.shape[1] // 128)]


def score_kernel(e_ref, coef_ref, s_ref, lse_ref):
    rows = score_tile(e_ref, coef_ref, s_ref)
    for i, row in enumerate(rows):
        lse_ref[pl.ds(pl.program_id(0) * len(rows) + i, 1), :] = row


def score_kernel_b(e_ref, coef_ref, other_ref, keep_ref, s_ref, pay_ref):
    rows = score_tile(e_ref, coef_ref, s_ref)
    half = other_ref.shape[0]

    @pl.when(pl.program_id(0) == 0)
    def _():
        row = lax.broadcasted_iota(jnp.int32, (half, 128), 0)
        pay_ref[half:, :] = jnp.where(row == 0, keep_ref[...], 0.0)

    for i, row in enumerate(rows):
        at = pl.ds(pl.program_id(0) * len(rows) + i, 1)
        other = other_ref[at, :]
        top = jnp.maximum(row, other)
        pay_ref[at, :] = top + jnp.log(jnp.exp(row - top) + jnp.exp(other - top))


def moment_body(pay_ref, s_ref, e_ref, out_ref, p_ref):
    groups, _, _ = pay_ref.shape
    half = pay_ref.shape[1] // 2
    comps = s_ref.shape[0]
    width = e_ref.shape[1]
    pay = pay_ref[:, :half, :]
    top = jnp.max(pay, axis=0)
    lse = top + jnp.log(jnp.sum(jnp.exp(pay - top[None]), axis=0))
    total = jnp.zeros((comps, 128), F32)
    kept = jnp.zeros((1, 128), F32)
    for j in range(half):
        at = slice(j * 128, (j + 1) * 128)
        keep = pay_ref[2 * j, half : half + 1, :] + pay_ref[2 * j + 1, half : half + 1, :]
        p = (jnp.exp(s_ref[:, at] - lse[j : j + 1, :]) * keep).astype(BF16)
        p_ref[:, at] = p
        total = total + p.astype(F32)
        kept = kept + keep
    counts = jnp.sum(total, axis=1, keepdims=True)
    kept = jnp.broadcast_to(jnp.sum(kept, axis=1, keepdims=True), (comps, 1))
    rows = e_ref[...]
    p = p_ref[...]
    second = jnp.dot(p, square(rows), preferred_element_type=F32)
    first = jnp.dot(p, rows, preferred_element_type=F32)
    zero = jnp.zeros_like(counts)
    ext = lanes([counts, zero, kept, zero], comps)
    if out_ref.dtype == BF16:
        ext = split_ext(ext)
    out_ref[:, :width] = second.astype(out_ref.dtype)
    out_ref[:, width : 2 * width] = first.astype(out_ref.dtype)
    out_ref[:, 2 * width :] = ext
    return lse


def moment_kernel_b(pay_ref, s_ref, e_ref, out_ref, lse_ref, p_ref):
    lse_ref[...] = moment_body(pay_ref, s_ref, e_ref, out_ref, p_ref)


def moment_kernel(pay_ref, s_ref, e_ref, out_ref, p_ref):
    moment_body(pay_ref, s_ref, e_ref, out_ref, p_ref)


def to_bf16(out_ref, total):
    feats = total.shape[1] - EXT
    out_ref[:, :feats] = total[:, :feats].astype(BF16)
    out_ref[:, feats:] = split_ext(total[:, feats:])


def core_sum_kernel(own_ref, got_ref, up_ref, down_ref, mine_ref):
    rows = mine_ref.shape[0]
    half = rows // 2
    mine_ref[...] = own_ref[:rows, :] + got_ref[:rows, :].astype(F32)
    for i, ref in enumerate((up_ref, down_ref)):
        at = slice(rows + i * half, rows + (i + 1) * half)
        to_bf16(ref, own_ref[at, :] + got_ref[at, :].astype(F32))


def pair_sum_kernel(me_ref, mine_ref, low_ref, high_ref, own_ref, s1_ref, s2_ref, s3_ref, all_ref):
    half = low_ref.shape[0]
    quarter = own_ref.shape[0]
    all_ref[:half, :] = mine_ref[:half, :] + low_ref[...].astype(F32)
    all_ref[half:, :] = mine_ref[half:, :] + high_ref[...].astype(F32)
    me = me_ref[0]

    def rows(shift):
        return all_ref[pl.ds(lax.rem(me + shift, 4) * quarter, quarter), :]

    own_ref[...] = rows(0)
    for shift, ref in ((1, s1_ref), (2, s2_ref), (3, s3_ref)):
        to_bf16(ref, rows(shift))


def finish_kernel(n_comps, own_ref, g1_ref, g2_ref, g3_ref, out_ref):
    total = own_ref[...] + g1_ref[...].astype(F32) + g2_ref[...].astype(F32) + g3_ref[...].astype(F32)
    rows = total.shape[0]
    width = (total.shape[1] - EXT) // 2
    second, first, ext = total[:, :width], total[:, width : 2 * width], total[:, 2 * width :]
    counts = ext[:, 0:1] + ext[:, 1:2]
    kept = ext[:, 2:3] + ext[:, 3:4]
    denom = counts + 1.0
    mean = first / denom
    out_ref[:, :width] = mean.astype(BF16)
    out_ref[:, width : 2 * width] = (
        (second - 2.0 * mean * first + mean * mean * counts + 1.0) / denom
    ).astype(BF16)
    log_w = jnp.log(denom / (kept + float(n_comps)))
    out_ref[:, 2 * width :] = lanes(parts(log_w, 3), rows).astype(BF16)


def place_kernel(me_ref, r0_ref, r1_ref, r2_ref, r3_ref, mean_ref, var_ref, log_ref):
    quarter = r0_ref.shape[0]
    width = mean_ref.shape[1]
    me = me_ref[0]
    for shift, ref in enumerate((r0_ref, r1_ref, r2_ref, r3_ref)):
        at = pl.ds(lax.rem(me + 4 - shift, 4) * quarter, quarter)
        mean_ref[at, :] = ref[:, :width].astype(F32)
        var_ref[at, :] = ref[:, width : 2 * width].astype(F32)
        log_ref[at, :] = jnp.sum(ref[:, 2 * width :].astype(F32), axis=1, keepdims=True)


def ring(n, shift):
    return [(i, (i + shift) % n) for i in range(n)]


def local(embeddings, keep, means, variances, log_weights):
    own, width = embeddings.shape
    comps = means.shape[0]
    n_comps = comps * 64
    cols = 2 * width + EXT
    plane, z, core = ("x", "y"), ("zh", "zl"), "c"
    n_rows = 16 * own
    zh = lax.axis_index("zh").astype(jnp.int32).reshape(1)
    at = lax.axis_index(plane)

    coef = call(coef_kernel, sds((comps, cols), BF16), 3)(means, variances, log_weights[:, None])
    half = comps // 2
    low = lax.ppermute(coef[:half], z, ring(8, 1))
    high = lax.ppermute(coef[half:], z, ring(8, 7))

    rows = lax.all_to_all(
        jnp.broadcast_to(embeddings[None], (16, own, width)), plane, 0, 0
    ).reshape(n_rows, width)

    coef_a = jnp.concatenate([coef, low, high], axis=0)
    coef_b = lax.ppermute(coef_a, core, ring(2, 1))

    flag = keep.astype(F32)
    odd = (at % 2).astype(F32)
    flag = jnp.concatenate([flag * (1.0 - odd), flag * odd]).reshape(1, 2 * own)

    tile = 256
    grid = n_rows // tile
    score_flops = 2 * 2 * comps * n_rows * 2 * width
    e_spec = pl.BlockSpec((tile, width), lambda i: (i, 0))
    s_spec = pl.BlockSpec((2 * comps, tile), lambda i: (0, i))
    s_shape = sds((2 * comps, n_rows), F32)

    def whole(shape):
        return pl.BlockSpec(shape, lambda i: (0,) * len(shape))

    lse_rows = n_rows // 128
    score_a, lse_a = call(
        score_kernel,
        (s_shape, sds((lse_rows, 128), F32)),
        2,
        score_flops,
        grid=(grid,),
        in_specs=[e_spec, whole((2 * comps, cols))],
        out_specs=[s_spec, whole((lse_rows, 128))],
    )(rows, coef_a)
    score_b, pay = call(
        score_kernel_b,
        (s_shape, sds((2 * lse_rows, 128), F32)),
        4,
        score_flops,
        grid=(grid,),
        in_specs=[e_spec, whole((2 * comps, cols)), whole((lse_rows, 128)), whole((1, 128))],
        out_specs=[s_spec, whole((2 * lse_rows, 128))],
    )(rows, coef_b, lse_a, flag)

    pays = lax.all_to_all(jnp.broadcast_to(pay[None], (16,) + pay.shape), plane, 0, 0)

    p_scratch = dict(scratch_shapes=[pltpu.VMEM((2 * comps, n_rows), BF16)])
    send, lse = call(
        moment_kernel_b,
        (sds((2 * comps, cols), BF16), sds((lse_rows, 128), F32)),
        3,
        score_flops,
        **p_scratch,
    )(pays, score_b, rows)
    got = lax.ppermute(send, core, ring(2, 1))
    own_sum = call(moment_kernel, sds((2 * comps, cols), F32), 3, score_flops, **p_scratch)(
        pays, score_a, rows
    )
    up, down, mine = call(
        core_sum_kernel,
        (sds((half, cols), BF16), sds((half, cols), BF16), sds((comps, cols), F32)),
        2,
    )(own_sum, got)
    low = lax.ppermute(up, z, ring(8, 1))
    high = lax.ppermute(down, z, ring(8, 7))
    quarter = comps // 4
    q32, q16 = sds((quarter, cols), F32), sds((quarter, cols), BF16)
    own_q, s1, s2, s3 = call(
        pair_sum_kernel,
        (q32, q16, q16, q16),
        4,
        smem=(0,),
        scratch_shapes=[pltpu.VMEM((comps, cols), F32)],
    )(zh, mine, low, high)
    g = [lax.ppermute(s, "zh", ring(4, i + 1)) for i, s in enumerate((s1, s2, s3))]
    result = call(functools.partial(finish_kernel, n_comps), q16, 4)(own_q, *g)
    r = [result] + [lax.ppermute(result, "zh", ring(4, s)) for s in (1, 2, 3)]
    out = sds((comps, width), F32)
    new_means, new_vars, new_log = call(
        place_kernel, (out, out, sds((comps, 1), F32)), 5, smem=(0,)
    )(zh, *r)

    own_lse = lax.dynamic_slice_in_dim(lse.reshape(-1), at * own, own)
    wide = embeddings.astype(F32)
    log_lik = own_lse + 0.5 * jnp.sum(wide * wide, axis=1) + 0.5 * width * math.log(2.0 * math.pi)
    return new_means, new_vars, new_log.reshape(-1), log_lik


def solution(mesh):
    axes = ("x", "y", "zl", "c")
    fine = Mesh(mesh.devices.reshape(4, 4, 4, 2, 2), ("zh",) + axes)
    both = ("zh",) + axes
    return jax.shard_map(
        local,
        mesh=fine,
        in_specs=(P(both, None), P(both), P(axes, None), P(axes, None), P(axes)),
        out_specs=(P(axes, None), P(axes, None), P(axes), P(both)),
        check_vma=False,
    )
```

```python
import functools
import math

import jax
import jax.numpy as jnp
from jax import lax
from jax.experimental import pallas as pl
from jax.experimental.pallas import tpu as pltpu
from jax.sharding import Mesh, PartitionSpec as P

F32 = jnp.float32
BF16 = jnp.bfloat16
EXT = 128
VMEM = pl.BlockSpec(memory_space=pltpu.VMEM)
SMEM = pl.BlockSpec(memory_space=pltpu.SMEM)
NT = (((1,), (1,)), ((), ()))
SHIFTS = (0, 1, 3, 2)
INTERPRET = False


def call(kernel, out_shape, n_in, flops=0, nbytes=0, smem=(), **kw):
    many = isinstance(out_shape, (list, tuple))
    n_out = len(out_shape) if many else 1
    specs = dict(
        in_specs=[SMEM if i in smem else VMEM for i in range(n_in)],
        out_specs=[VMEM] * n_out if many else VMEM,
    )
    specs.update(kw)
    return pl.pallas_call(
        kernel,
        out_shape=out_shape,
        compiler_params=pltpu.CompilerParams(vmem_limit_bytes=40 * 2**20),
        cost_estimate=pl.CostEstimate(flops=flops, bytes_accessed=nbytes, transcendentals=0),
        interpret=INTERPRET,
        **specs,
    )


def sds(shape, dtype):
    return jax.ShapeDtypeStruct(shape, dtype)


def parts(col, n):
    out = []
    for _ in range(n):
        top = col.astype(BF16).astype(F32)
        out.append(top)
        col = col - top
    return out


def lanes(cols, rows):
    lane = lax.broadcasted_iota(jnp.int32, (rows, EXT), 1)
    ext = jnp.zeros((rows, EXT), F32)
    for i, col in enumerate(cols):
        ext = jnp.where(lane == i, col, ext)
    return ext


def split_ext(ext):
    counts = ext[:, 0:1] + ext[:, 1:2]
    kept = ext[:, 2:3] + ext[:, 3:4]
    return lanes(parts(counts, 2) + parts(kept, 2), ext.shape[0]).astype(BF16)


def coef_kernel(m_ref, v_ref, w_ref, out_ref):
    rows, width = m_ref.shape
    m, v = m_ref[...], v_ref[...]
    prec = 1.0 / v
    out_ref[:, :width] = (-0.5 * prec).astype(BF16)
    out_ref[:, width : 2 * width] = (m * prec).astype(BF16)
    offset = (
        w_ref[...]
        - 0.5 * jnp.sum(m * m * prec + jnp.log(v), axis=1, keepdims=True)
        - 0.5 * width * math.log(2.0 * math.pi)
    )
    out_ref[:, 2 * width :] = lanes(parts(offset, 3), rows).astype(BF16)


def square(rows):
    wide = rows.astype(F32)
    return (wide * wide).astype(BF16)


def slot(ids_ref, piece, k):
    return lax.rem(ids_ref[0] + 4 - SHIFTS[k], 4) * 4 + lax.rem(ids_ref[1] + 4 - SHIFTS[piece], 4)


def score_kernel(e_ref, coef_a_ref, coef_b_ref, s_a_ref, s_b_ref, lse_ref):
    width = e_ref.shape[1]
    rows = e_ref[...]
    squares = square(rows)
    tops = []
    for coef_ref, s_ref in ((coef_a_ref, s_a_ref), (coef_b_ref, s_b_ref)):
        s = lax.dot_general(coef_ref[:, :width], squares, NT, preferred_element_type=F32)
        s = s + lax.dot_general(coef_ref[:, width : 2 * width], rows, NT, preferred_element_type=F32)
        s = s + jnp.sum(coef_ref[:, 2 * width :].astype(F32), axis=1, keepdims=True)
        s_ref[...] = s
        tops.append(jnp.max(s, axis=0, keepdims=True))
    top = jnp.maximum(*tops)
    total = sum(jnp.sum(jnp.exp(ref[...] - top), axis=0, keepdims=True) for ref in (s_a_ref, s_b_ref))
    lse_ref[...] = top + jnp.log(total)


def pay_kernel(ids_ref, keep_ref, l0_ref, l1_ref, l2_ref, l3_ref, pay_ref):
    lane = lax.broadcasted_iota(jnp.int32, (1, 128), 1)
    for piece, ref in enumerate((l0_ref, l1_ref, l2_ref, l3_ref)):
        for k in range(4):
            row = ref[:, (k // 2) * 128 : (k // 2 + 1) * 128]
            if k % 2:
                row = pltpu.roll(row, 64, 1)
            pay_ref[pl.ds(slot(ids_ref, piece, k), 1), :] = jnp.where(lane < 64, row, 0.0)
    pay_ref[0:1, :] = jnp.where(lane < 64, pay_ref[0:1, :], keep_ref[...])


def moment_body(ids_ref, pay_ref, lse_ref, s_refs, e_refs, out_ref):
    comps = s_refs[0].shape[0]
    width = e_refs[0].shape[1]
    pay = pay_ref[...]
    top = jnp.max(pay, axis=0)
    lse_ref[...] = top + jnp.log(jnp.sum(jnp.exp(pay - top[None]), axis=0))
    lane = lax.broadcasted_iota(jnp.int32, (1, 128), 1)
    total = jnp.zeros((comps, 128), F32)
    kept = jnp.zeros((1, 128), F32)
    second = first = None
    for piece, (s_ref, e_ref) in enumerate(zip(s_refs, e_refs, strict=True)):
        ps = []
        for j in range(2):
            at = [slot(ids_ref, piece, 2 * j + i) for i in range(2)]
            left, right = (lse_ref[pl.ds(i, 1), :] for i in at)
            lse = jnp.where(lane < 64, left, pltpu.roll(right, 64, 1))
            left, right = (pay_ref[i, 0:1, :] for i in at)
            keep = jnp.where(lane < 64, pltpu.roll(left, 64, 1), right)
            p = (jnp.exp(s_ref[:, j * 128 : (j + 1) * 128] - lse) * keep).astype(BF16)
            total = total + p.astype(F32)
            kept = kept + keep
            ps.append(p)
        p = jnp.concatenate(ps, axis=1)
        rows = e_ref[...]
        add2 = jnp.dot(p, square(rows), preferred_element_type=F32)
        add1 = jnp.dot(p, rows, preferred_element_type=F32)
        second = add2 if piece == 0 else second + add2
        first = add1 if piece == 0 else first + add1
    counts = jnp.sum(total, axis=1, keepdims=True)
    kept = jnp.broadcast_to(jnp.sum(kept, axis=1, keepdims=True), (comps, 1))
    zero = jnp.zeros_like(counts)
    ext = lanes([counts, zero, kept, zero], comps)
    if out_ref.dtype == BF16:
        ext = split_ext(ext)
    out_ref[:, :width] = second.astype(out_ref.dtype)
    out_ref[:, width : 2 * width] = first.astype(out_ref.dtype)
    out_ref[:, 2 * width :] = ext


def moment_kernel_b(ids_ref, pay_ref, s0, s1, s2, s3, e0, e1, e2, e3, out_ref, own_ref, lse_ref):
    moment_body(ids_ref, pay_ref, lse_ref, (s0, s1, s2, s3), (e0, e1, e2, e3), out_ref)
    own_ref[...] = lse_ref[pl.ds(slot(ids_ref, 0, 0), 1), :]


def moment_kernel(ids_ref, pay_ref, s0, s1, s2, s3, e0, e1, e2, e3, out_ref, lse_ref):
    moment_body(ids_ref, pay_ref, lse_ref, (s0, s1, s2, s3), (e0, e1, e2, e3), out_ref)


def to_bf16(out_ref, total):
    feats = total.shape[1] - EXT
    out_ref[:, :feats] = total[:, :feats].astype(BF16)
    out_ref[:, feats:] = split_ext(total[:, feats:])


def core_sum_kernel(own_ref, got_ref, up_ref, down_ref, mine_ref):
    rows = mine_ref.shape[0]
    half = rows // 2
    mine_ref[...] = own_ref[:rows, :] + got_ref[:rows, :].astype(F32)
    for i, ref in enumerate((up_ref, down_ref)):
        at = slice(rows + i * half, rows + (i + 1) * half)
        to_bf16(ref, own_ref[at, :] + got_ref[at, :].astype(F32))


def pair_sum_kernel(me_ref, mine_ref, low_ref, high_ref, own_ref, s1_ref, s2_ref, s3_ref, all_ref):
    half = low_ref.shape[0]
    quarter = own_ref.shape[0]
    all_ref[:half, :] = mine_ref[:half, :] + low_ref[...].astype(F32)
    all_ref[half:, :] = mine_ref[half:, :] + high_ref[...].astype(F32)
    me = me_ref[2]

    def rows(shift):
        return all_ref[pl.ds(lax.rem(me + shift, 4) * quarter, quarter), :]

    own_ref[...] = rows(0)
    for shift, ref in ((1, s1_ref), (2, s2_ref), (3, s3_ref)):
        to_bf16(ref, rows(shift))


def finish_kernel(n_comps, own_ref, g1_ref, g2_ref, g3_ref, out_ref):
    total = own_ref[...] + g1_ref[...].astype(F32) + g2_ref[...].astype(F32) + g3_ref[...].astype(F32)
    rows = total.shape[0]
    width = (total.shape[1] - EXT) // 2
    second, first, ext = total[:, :width], total[:, width : 2 * width], total[:, 2 * width :]
    counts = ext[:, 0:1] + ext[:, 1:2]
    kept = ext[:, 2:3] + ext[:, 3:4]
    denom = counts + 1.0
    mean = first / denom
    out_ref[:, :width] = mean.astype(BF16)
    out_ref[:, width : 2 * width] = (
        (second - 2.0 * mean * first + mean * mean * counts + 1.0) / denom
    ).astype(BF16)
    log_w = jnp.log(denom / (kept + float(n_comps)))
    out_ref[:, 2 * width :] = lanes(parts(log_w, 3), rows).astype(BF16)


def place_kernel(me_ref, r0_ref, r1_ref, r2_ref, r3_ref, mean_ref, var_ref, log_ref, ext_ref):
    quarter = r0_ref.shape[0]
    width = mean_ref.shape[1]
    me = me_ref[2]
    for shift, ref in enumerate((r0_ref, r1_ref, r2_ref, r3_ref)):
        at = pl.ds(lax.rem(me + 4 - shift, 4) * quarter, quarter)
        mean_ref[at, :] = ref[:, :width].astype(F32)
        var_ref[at, :] = ref[:, width : 2 * width].astype(F32)
        ext_ref[at, :] = ref[:, 2 * width :].astype(F32)
    ones = jnp.ones((8, EXT), BF16)
    log_ref[...] = lax.dot_general(ones, ext_ref[...].astype(BF16), NT, preferred_element_type=F32)[0:1, :]


def ring(n, shift):
    return [(i, (i + shift) % n) for i in range(n)]


def local(embeddings, keep, means, variances, log_weights):
    own, width = embeddings.shape
    comps = means.shape[0]
    n_comps = comps * 64
    cols = 2 * width + EXT
    plane, z, core = ("x", "y"), ("zh", "zl"), "c"
    ids = jnp.stack([lax.axis_index(a) for a in ("x", "y", "zh")]).astype(jnp.int32)

    line = [embeddings] + [lax.ppermute(embeddings, "x", ring(4, s)) for s in SHIFTS[1:]]
    line = jnp.concatenate(line, axis=0)
    pieces = [line] + [lax.ppermute(line, "y", ring(4, s)) for s in SHIFTS[1:]]

    coef = call(coef_kernel, sds((comps, cols), BF16), 3)(means, variances, log_weights[:, None])
    coef_a = jnp.concatenate([coef, lax.ppermute(coef, "zl", ring(2, 1))], axis=0)
    coef_b = lax.ppermute(coef_a, core, ring(2, 1))

    tile = 4 * own
    flops = 2 * 2 * comps * tile * 2 * width
    half_s = sds((2 * comps, tile), F32)
    scores = [
        call(score_kernel, (half_s, half_s, sds((1, tile), F32)), 3, 2 * flops)(p, coef_a, coef_b)
        for p in pieces
    ]
    flag = jnp.pad(keep.astype(F32), (own, 0)).reshape(1, 2 * own)
    pay = call(pay_kernel, sds((16, 128), F32), 6, smem=(0,))(ids, flag, *[s[2] for s in scores])
    pays = lax.all_to_all(jnp.broadcast_to(pay[None], (16,) + pay.shape), plane, 0, 0)

    lse_scratch = dict(smem=(0,), scratch_shapes=[pltpu.VMEM((16, 128), F32)])
    send, own_lse = call(
        moment_kernel_b, (sds((2 * comps, cols), BF16), sds((1, 128), F32)), 10, 4 * flops, **lse_scratch
    )(ids, pays, *[s[1] for s in scores], *pieces)
    got = lax.ppermute(send, core, ring(2, 1))
    own_sum = call(moment_kernel, sds((2 * comps, cols), F32), 10, 4 * flops, **lse_scratch)(
        ids, pays, *[s[0] for s in scores], *pieces
    )
    half = comps // 2
    up, down, mine = call(
        core_sum_kernel,
        (sds((half, cols), BF16), sds((half, cols), BF16), sds((comps, cols), F32)),
        2,
    )(own_sum, got)
    low = lax.ppermute(up, z, ring(8, 1))
    high = lax.ppermute(down, z, ring(8, 7))
    quarter = comps // 4
    q32, q16 = sds((quarter, cols), F32), sds((quarter, cols), BF16)
    own_q, s1, s2, s3 = call(
        pair_sum_kernel,
        (q32, q16, q16, q16),
        4,
        smem=(0,),
        scratch_shapes=[pltpu.VMEM((comps, cols), F32)],
    )(ids, mine, low, high)
    g = [lax.ppermute(s, "zh", ring(4, i)) for i, s in ((2, s2), (1, s1), (3, s3))]
    result = call(functools.partial(finish_kernel, n_comps), q16, 4)(own_q, *g)
    r2, r1, r3 = [lax.ppermute(result, "zh", ring(4, s)) for s in (2, 1, 3)]
    out = sds((comps, width), F32)
    new_means, new_vars, new_log = call(
        place_kernel,
        (out, out, sds((1, comps), F32)),
        5,
        smem=(0,),
        scratch_shapes=[pltpu.VMEM((comps, EXT), F32)],
    )(ids, result, r1, r2, r3)

    wide = embeddings.astype(F32)
    own_norm = 0.5 * jnp.sum(wide * wide, axis=1) + 0.5 * width * math.log(2.0 * math.pi)
    return new_means, new_vars, new_log.reshape(-1), own_lse[0, :own] + own_norm


def solution(mesh):
    axes = ("x", "y", "zl", "c")
    fine = Mesh(mesh.devices.reshape(4, 4, 4, 2, 2), ("zh",) + axes)
    both = ("zh",) + axes
    return jax.shard_map(
        local,
        mesh=fine,
        in_specs=(P(both, None), P(both), P(axes, None), P(axes, None), P(axes)),
        out_specs=(P(axes, None), P(axes, None), P(axes), P(both)),
        check_vma=False,
    )
```

```python
import functools
import math

import jax
import jax.numpy as jnp
from jax import lax
from jax.experimental import pallas as pl
from jax.experimental.pallas import tpu as pltpu
from jax.sharding import Mesh, PartitionSpec as P

F32 = jnp.float32
BF16 = jnp.bfloat16
EXT = 128
VMEM = pl.BlockSpec(memory_space=pltpu.VMEM)
NT = (((1,), (1,)), ((), ()))
SHIFTS = (0, 1, 3, 2)
SLOTS = (
    tuple((s, 0) for s in SHIFTS),
    ((0, 1), (0, 3), (1, 1), (1, 3)),
    ((3, 1), (3, 3), (2, 1), (2, 3)),
    tuple((s, 2) for s in SHIFTS),
)
INTERPRET = False


def call(kernel, out_shape, n_in, flops=0, nbytes=0, **kw):
    many = isinstance(out_shape, (list, tuple))
    n_out = len(out_shape) if many else 1
    specs = dict(
        in_specs=[VMEM] * n_in,
        out_specs=[VMEM] * n_out if many else VMEM,
    )
    specs.update(kw)
    return pl.pallas_call(
        kernel,
        out_shape=out_shape,
        compiler_params=pltpu.CompilerParams(vmem_limit_bytes=16 * 2**20),
        cost_estimate=pl.CostEstimate(flops=flops, bytes_accessed=nbytes, transcendentals=0),
        interpret=INTERPRET,
        **specs,
    )


def sds(shape, dtype):
    return jax.ShapeDtypeStruct(shape, dtype)


def parts(col, n):
    out = []
    for _ in range(n):
        top = col.astype(BF16).astype(F32)
        out.append(top)
        col = col - top
    return out


def lanes(cols, rows):
    lane = lax.broadcasted_iota(jnp.int32, (rows, EXT), 1)
    ext = jnp.zeros((rows, EXT), F32)
    for i, col in enumerate(cols):
        ext = jnp.where(lane == i, col, ext)
    return ext


def split_ext(ext):
    counts = ext[:, 0:1] + ext[:, 1:2]
    kept = ext[:, 2:3] + ext[:, 3:4]
    return lanes(parts(counts, 2) + parts(kept, 2), ext.shape[0]).astype(BF16)


def coef_kernel(m_ref, v_ref, w_ref, out_ref):
    rows, width = m_ref.shape
    m, v = m_ref[...], v_ref[...]
    prec = 1.0 / v
    out_ref[:, :width] = (-0.5 * prec).astype(BF16)
    out_ref[:, width : 2 * width] = (m * prec).astype(BF16)
    down = lax.broadcasted_iota(jnp.int32, (rows, rows), 0)
    across = lax.broadcasted_iota(jnp.int32, (rows, rows), 1)
    offset = (
        jnp.sum(jnp.where(down == across, w_ref[...], 0.0), axis=1, keepdims=True)
        - 0.5 * jnp.sum(m * m * prec + jnp.log(v), axis=1, keepdims=True)
        - 0.5 * width * math.log(2.0 * math.pi)
    )
    out_ref[:, 2 * width :] = lanes(parts(offset, 3), rows).astype(BF16)


def square(rows):
    wide = rows.astype(F32)
    return (wide * wide).astype(BF16)


def slot(group, k):
    back_x, back_y = SLOTS[group][k]
    x, y = lax.axis_index("x"), lax.axis_index("y")
    return lax.rem(x + 4 - back_x, 4) * 4 + lax.rem(y + 4 - back_y, 4)


def joined(refs):
    return refs[0][...] if len(refs) == 1 else jnp.concatenate([r[...] for r in refs], axis=0)


def score_kernel(*refs):
    *e_refs, coef_ref, s_ref, lse_ref = refs
    rows = joined(e_refs)
    width = rows.shape[1]
    s = lax.dot_general(coef_ref[:, :width], square(rows), NT, preferred_element_type=F32)
    s = s + lax.dot_general(coef_ref[:, width : 2 * width], rows, NT, preferred_element_type=F32)
    s = s + jnp.sum(coef_ref[:, 2 * width :].astype(F32), axis=1, keepdims=True)
    s_ref[...] = s
    top = jnp.max(s, axis=0, keepdims=True)
    lse_ref[...] = top + jnp.log(jnp.sum(jnp.exp(s - top), axis=0, keepdims=True))


def pay_kernel(keep_ref, *refs):
    *lse_refs, pay_ref = refs
    lane = lax.broadcasted_iota(jnp.int32, (1, 128), 1)
    for group in range(4):
        a, b = lse_refs[group][...], lse_refs[4 + group][...]
        top = jnp.maximum(a, b)
        both = top + jnp.log(jnp.exp(a - top) + jnp.exp(b - top))
        for k in range(4):
            row = both[:, (k // 2) * 128 : (k // 2 + 1) * 128]
            if k % 2:
                row = pltpu.roll(row, 64, 1)
            pay_ref[pl.ds(slot(group, k), 1), :] = jnp.where(lane < 64, row, 0.0)
    pay_ref[0:1, :] = jnp.where(lane < 64, pay_ref[0:1, :], keep_ref[...])


def moment_body(pay_ref, lse_ref, s_refs, e_refs, out_ref):
    comps = s_refs[0].shape[0]
    width = e_refs[0][0].shape[1]
    pay = pay_ref[...]
    top = jnp.max(pay, axis=0)
    lse_ref[...] = top + jnp.log(jnp.sum(jnp.exp(pay - top[None]), axis=0))
    lane = lax.broadcasted_iota(jnp.int32, (1, 128), 1)
    total = jnp.zeros((comps, 128), F32)
    kept = jnp.zeros((1, 128), F32)
    second = first = None
    for group, (s_ref, e_group) in enumerate(zip(s_refs, e_refs, strict=True)):
        ps = []
        for j in range(2):
            at = [slot(group, 2 * j + i) for i in range(2)]
            left, right = (lse_ref[pl.ds(i, 1), :] for i in at)
            lse = jnp.where(lane < 64, left, pltpu.roll(right, 64, 1))
            left, right = (pay_ref[i, 0:1, :] for i in at)
            keep = jnp.where(lane < 64, pltpu.roll(left, 64, 1), right)
            p = (jnp.exp(s_ref[:, j * 128 : (j + 1) * 128] - lse) * keep).astype(BF16)
            total = total + p.astype(F32)
            kept = kept + keep
            ps.append(p)
        p = jnp.concatenate(ps, axis=1)
        rows = joined(e_group)
        add2 = jnp.dot(p, square(rows), preferred_element_type=F32)
        add1 = jnp.dot(p, rows, preferred_element_type=F32)
        second = add2 if group == 0 else second + add2
        first = add1 if group == 0 else first + add1
    counts = jnp.sum(total, axis=1, keepdims=True)
    kept = jnp.broadcast_to(jnp.sum(kept, axis=1, keepdims=True), (comps, 1))
    zero = jnp.zeros_like(counts)
    ext = lanes([counts, zero, kept, zero], comps)
    if out_ref.dtype == BF16:
        ext = split_ext(ext)
    out_ref[:, :width] = second.astype(out_ref.dtype)
    out_ref[:, width : 2 * width] = first.astype(out_ref.dtype)
    out_ref[:, 2 * width :] = ext


def moment_refs(refs):
    pay_ref, s0, s1, s2, s3, e0, e1, e2, e3, e4, e5 = refs
    return pay_ref, (s0, s1, s2, s3), ((e0,), (e1, e2), (e3, e4), (e5,))


def moment_kernel_b(*refs):
    *refs, out_ref, own_ref, lse_ref = refs
    pay_ref, s_refs, e_refs = moment_refs(refs)
    moment_body(pay_ref, lse_ref, s_refs, e_refs, out_ref)
    own_ref[...] = lse_ref[pl.ds(slot(0, 0), 1), :]


def moment_kernel(*refs):
    *refs, out_ref, lse_ref = refs
    pay_ref, s_refs, e_refs = moment_refs(refs)
    moment_body(pay_ref, lse_ref, s_refs, e_refs, out_ref)


def to_bf16(out_ref, total):
    feats = total.shape[1] - EXT
    out_ref[:, :feats] = total[:, :feats].astype(BF16)
    out_ref[:, feats:] = split_ext(total[:, feats:])


def core_sum_kernel(own_ref, got_ref, up_ref, down_ref, mine_ref):
    rows = mine_ref.shape[0]
    half = rows // 2
    mine_ref[...] = own_ref[:rows, :] + got_ref[:rows, :].astype(F32)
    for i, ref in enumerate((up_ref, down_ref)):
        at = slice(rows + i * half, rows + (i + 1) * half)
        to_bf16(ref, own_ref[at, :] + got_ref[at, :].astype(F32))


def pair_sum_kernel(mine_ref, low_ref, high_ref, own_ref, s1_ref, s2_ref, s3_ref, all_ref):
    half = low_ref.shape[0]
    quarter = own_ref.shape[0]
    all_ref[:half, :] = mine_ref[:half, :] + low_ref[...].astype(F32)
    all_ref[half:, :] = mine_ref[half:, :] + high_ref[...].astype(F32)
    me = lax.axis_index("zh")

    def rows(shift):
        return all_ref[pl.ds(lax.rem(me + shift, 4) * quarter, quarter), :]

    own_ref[...] = rows(0)
    for shift, ref in ((1, s1_ref), (2, s2_ref), (3, s3_ref)):
        to_bf16(ref, rows(shift))


def finish_kernel(n_comps, own_ref, g1_ref, g2_ref, g3_ref, out_ref):
    total = own_ref[...] + g1_ref[...].astype(F32) + g2_ref[...].astype(F32) + g3_ref[...].astype(F32)
    rows = total.shape[0]
    width = (total.shape[1] - EXT) // 2
    second, first, ext = total[:, :width], total[:, width : 2 * width], total[:, 2 * width :]
    counts = ext[:, 0:1] + ext[:, 1:2]
    kept = ext[:, 2:3] + ext[:, 3:4]
    denom = counts + 1.0
    mean = first / denom
    out_ref[:, :width] = mean.astype(BF16)
    out_ref[:, width : 2 * width] = (
        (second - 2.0 * mean * first + mean * mean * counts + 1.0) / denom
    ).astype(BF16)
    log_w = jnp.log(denom / (kept + float(n_comps)))
    out_ref[:, 2 * width :] = lanes(parts(log_w, 3), rows).astype(BF16)


def place_kernel(r0_ref, r2_ref, r1_ref, r3_ref, mean_ref, var_ref, log_ref, ext_ref):
    quarter = r0_ref.shape[0]
    width = mean_ref.shape[1]
    me = lax.axis_index("zh")
    for shift, ref in enumerate((r0_ref, r1_ref, r2_ref, r3_ref)):
        at = pl.ds(lax.rem(me + 4 - shift, 4) * quarter, quarter)
        mean_ref[at, :] = ref[:, :width].astype(F32)
        var_ref[at, :] = ref[:, width : 2 * width].astype(F32)
        ext_ref[at, :] = ref[:, 2 * width :].astype(F32)
    ones = jnp.ones((8, EXT), BF16)
    log_ref[...] = lax.dot_general(ones, ext_ref[...].astype(BF16), NT, preferred_element_type=F32)[0:1, :]


def ring(n, shift):
    return [(i, (i + shift) % n) for i in range(n)]


def local(embeddings, keep, means, variances, log_weights):
    own, width = embeddings.shape
    comps = means.shape[0]
    n_comps = comps * 64
    cols = 2 * width + EXT
    plane, z, core = ("x", "y"), ("zh", "zl"), "c"

    back_y = [lax.ppermute(embeddings, "y", ring(4, s)) for s in (1, 3)]
    line = [embeddings] + [lax.ppermute(embeddings, "x", ring(4, s)) for s in SHIFTS[1:]]
    line = jnp.concatenate(line, axis=0)
    pair = jnp.concatenate(back_y, axis=0)

    coef = call(coef_kernel, sds((comps, cols), BF16), 3, 4 * 2**20, 2 * 2**20)(
        means, variances, log_weights[None, :]
    )
    coef, pair = lax.optimization_barrier((coef, pair))
    coef_a = jnp.concatenate([coef, lax.ppermute(coef, "zl", ring(2, 1))], axis=0)
    far = lax.ppermute(line, "y", ring(4, 2))
    rest = [lax.ppermute(pair, "x", ring(4, s)) for s in SHIFTS[1:]]
    coef_a, far, rest = lax.optimization_barrier((coef_a, far, rest))
    coef_b = lax.ppermute(coef_a, core, ring(2, 1))

    groups = [[line], [pair, rest[0]], [rest[1], rest[2]], [far]]
    pieces = [e for group in groups for e in group]
    tile = 4 * own
    flops = 2 * 2 * comps * tile * 2 * width
    half_s = sds((2 * comps, tile), F32)
    scores_a, scores_b = (
        [
            call(score_kernel, (half_s, sds((1, tile), F32)), 1 + len(group), flops)(*group, coef)
            for group in groups
        ]
        for coef in (coef_a, coef_b)
    )
    flag = jnp.pad(keep.astype(F32), (own, 0)).reshape(1, 2 * own)
    pay = call(pay_kernel, sds((16, 128), F32), 9)(
        flag, *[s[1] for s in scores_a + scores_b]
    )
    pays = lax.all_to_all(jnp.broadcast_to(pay[None], (16,) + pay.shape), plane, 0, 0)

    lse_scratch = dict(scratch_shapes=[pltpu.VMEM((16, 128), F32)])
    send, own_lse = call(
        moment_kernel_b, (sds((2 * comps, cols), BF16), sds((1, 128), F32)), 11, 4 * flops, **lse_scratch
    )(pays, *[s[0] for s in scores_b], *pieces)
    got = lax.ppermute(send, core, ring(2, 1))
    own_sum = call(moment_kernel, sds((2 * comps, cols), F32), 11, 4 * flops, **lse_scratch)(
        pays, *[s[0] for s in scores_a], *pieces
    )
    half = comps // 2
    up, down, mine = call(
        core_sum_kernel,
        (sds((half, cols), BF16), sds((half, cols), BF16), sds((comps, cols), F32)),
        2,
    )(own_sum, got)
    low = lax.ppermute(up, z, ring(8, 1))
    high = lax.ppermute(down, z, ring(8, 7))
    quarter = comps // 4
    q32, q16 = sds((quarter, cols), F32), sds((quarter, cols), BF16)
    own_q, s1, s2, s3 = call(
        pair_sum_kernel,
        (q32, q16, q16, q16),
        3,
        scratch_shapes=[pltpu.VMEM((comps, cols), F32)],
    )(mine, low, high)
    g = [lax.ppermute(s, "zh", ring(4, i)) for i, s in ((2, s2), (1, s1), (3, s3))]
    result = call(functools.partial(finish_kernel, n_comps), q16, 4)(own_q, *g)
    r2, r1, r3 = [lax.ppermute(result, "zh", ring(4, s)) for s in (2, 1, 3)]
    out = sds((comps, width), F32)
    new_means, new_vars, new_log = call(
        place_kernel,
        (out, out, sds((1, comps), F32)),
        4,
        scratch_shapes=[pltpu.VMEM((comps, EXT), F32)],
    )(result, r2, r1, r3)

    wide = embeddings.astype(F32)
    own_norm = 0.5 * jnp.sum(wide * wide, axis=1) + 0.5 * width * math.log(2.0 * math.pi)
    return new_means, new_vars, new_log.reshape(-1), own_lse[0, :own] + own_norm


def solution(mesh):
    axes = ("x", "y", "zl", "c")
    fine = Mesh(mesh.devices.reshape(4, 4, 4, 2, 2), ("zh",) + axes)
    both = ("zh",) + axes
    return jax.shard_map(
        local,
        mesh=fine,
        in_specs=(P(both, None), P(both), P(axes, None), P(axes, None), P(axes)),
        out_specs=(P(axes, None), P(axes, None), P(axes), P(both)),
        check_vma=False,
    )
```

```python
import functools
import math

import jax
import jax.numpy as jnp
from jax import lax
from jax.experimental import pallas as pl
from jax.experimental.pallas import tpu as pltpu
from jax.sharding import Mesh, PartitionSpec as P

F32 = jnp.float32
BF16 = jnp.bfloat16
EXT = 128
VMEM = pl.BlockSpec(memory_space=pltpu.VMEM)
NT = (((1,), (1,)), ((), ()))
SHIFTS = (0, 1, 3, 2)
SLOTS = (
    tuple((s, 0) for s in SHIFTS),
    ((0, 1), (0, 3), (1, 1), (1, 3)),
    ((3, 1), (3, 3), (2, 1), (2, 3)),
    tuple((s, 2) for s in SHIFTS),
)
DROPPED = 1e30
INTERPRET = False


def call(kernel, out_shape, n_in, flops=0, nbytes=0, **kw):
    many = isinstance(out_shape, (list, tuple))
    n_out = len(out_shape) if many else 1
    specs = dict(
        in_specs=[VMEM] * n_in,
        out_specs=[VMEM] * n_out if many else VMEM,
    )
    specs.update(kw)
    return pl.pallas_call(
        kernel,
        out_shape=out_shape,
        compiler_params=pltpu.CompilerParams(vmem_limit_bytes=16 * 2**20),
        cost_estimate=pl.CostEstimate(flops=flops, bytes_accessed=nbytes, transcendentals=0),
        interpret=INTERPRET,
        **specs,
    )


def sds(shape, dtype):
    return jax.ShapeDtypeStruct(shape, dtype)


def parts(col, n):
    out = []
    for _ in range(n):
        top = col.astype(BF16).astype(F32)
        out.append(top)
        col = col - top
    return out


def lanes(cols, rows):
    lane = lax.broadcasted_iota(jnp.int32, (rows, EXT), 1)
    ext = jnp.zeros((rows, EXT), F32)
    for i, col in enumerate(cols):
        ext = jnp.where(lane == i, col, ext)
    return ext


def split_ext(ext):
    counts = ext[:, 0:1] + ext[:, 1:2]
    kept = ext[:, 2:3] + ext[:, 3:4]
    return lanes(parts(counts, 2) + parts(kept, 2), ext.shape[0]).astype(BF16)


def coef_kernel(m_ref, v_ref, w_ref, out_ref):
    rows, width = m_ref.shape
    m, v = m_ref[...], v_ref[...]
    prec = 1.0 / v
    out_ref[:, :width] = (-0.5 * prec).astype(BF16)
    out_ref[:, width : 2 * width] = (m * prec).astype(BF16)
    down = lax.broadcasted_iota(jnp.int32, (rows, rows), 0)
    across = lax.broadcasted_iota(jnp.int32, (rows, rows), 1)
    offset = (
        jnp.sum(jnp.where(down == across, w_ref[...], 0.0), axis=1, keepdims=True)
        - 0.5 * jnp.sum(m * m * prec + jnp.log(v), axis=1, keepdims=True)
        - 0.5 * width * math.log(2.0 * math.pi)
    )
    out_ref[:, 2 * width :] = lanes(parts(offset, 3), rows).astype(BF16)


def square(rows):
    wide = rows.astype(F32)
    return (wide * wide).astype(BF16)


def slot(group, k):
    back_x, back_y = SLOTS[group][k]
    x, y = lax.axis_index("x"), lax.axis_index("y")
    return lax.rem(x + 4 - back_x, 4) * 4 + lax.rem(y + 4 - back_y, 4)


def score_kernel(e0_ref, e1_ref, e2_ref, e3_ref, coef_ref, s_ref, lse_ref, feats_ref):
    rows, width = e0_ref.shape
    for i, e_ref in enumerate((e0_ref, e1_ref, e2_ref, e3_ref)):
        at = slice(i * rows, (i + 1) * rows)
        feats_ref[at, :width] = square(e_ref[...])
        feats_ref[at, width:] = e_ref[...]
        s = lax.dot_general(
            coef_ref[:, : 2 * width], feats_ref[at, :], NT, preferred_element_type=F32
        )
        s = s + jnp.sum(coef_ref[:, 2 * width :].astype(F32), axis=1, keepdims=True)
        s_ref[:, at] = s
        top = jnp.max(s, axis=0, keepdims=True)
        lse_ref[:, at] = top + jnp.log(jnp.sum(jnp.exp(s - top), axis=0, keepdims=True))


def pay_kernel(keep_ref, own_ref, other_ref, pay_ref, true_ref):
    lane = lax.broadcasted_iota(jnp.int32, (1, 128), 1)
    first = lax.axis_index("c") == 0
    for i in range(16):
        at = slice((i // 2) * 128, (i // 2 + 1) * 128)
        own, other = own_ref[:, at], other_ref[:, at]
        if i == 0:
            true_ref[...] = own
            own = jnp.where((lane < 64) & (keep_ref[...] == 0.0), DROPPED, own)
        left, right = jnp.where(first, own, other), jnp.where(first, other, own)
        if i % 2:
            left = pltpu.roll(left, 64, 1)
        else:
            right = pltpu.roll(right, 64, 1)
        pay_ref[pl.ds(slot(i // 4, i % 4), 1), :] = jnp.where(lane < 64, left, right)


def logsumexp(x):
    top = jnp.max(x, axis=0)
    return top + jnp.log(jnp.sum(jnp.exp(x - top[None]), axis=0))


def moment_body(at_comp, refs, lse_ref):
    pay_ref, s_refs, feats_refs = refs[0], refs[1:3], refs[3:5]
    comps = 128
    lse = logsumexp(pay_ref[...])
    lse_ref[0] = lse
    lse_ref[1] = pltpu.roll(lse, 64, 1)
    lane = lax.broadcasted_iota(jnp.int32, (1, 128), 1)
    core = lax.axis_index("c")
    total = jnp.zeros((comps, 128), F32)
    moments = None
    for i, (s_ref, feats_ref) in enumerate(zip(s_refs, feats_refs, strict=True)):
        half = core if i == 0 else 1 - core
        ps = []
        for j in range(8):
            left, right = (slot(j // 2, 2 * (j % 2) + k) for k in range(2))
            there = jnp.where(
                lane < 64, lse_ref[half, pl.ds(left, 1), :], lse_ref[1 - half, pl.ds(right, 1), :]
            )
            s = s_ref[at_comp : at_comp + comps, j * 128 : (j + 1) * 128]
            p = jnp.exp(s - there).astype(BF16)
            total = total + p.astype(F32)
            ps.append(p)
        add = jnp.dot(jnp.concatenate(ps, axis=1), feats_ref[...], preferred_element_type=F32)
        moments = add if i == 0 else moments + add
    counts = jnp.sum(total, axis=1, keepdims=True)
    kept = jnp.sum(jnp.where(lse < 0.5 * DROPPED, 1.0, 0.0), axis=(0, 1), keepdims=True)
    zero = jnp.zeros_like(counts)
    ext = lanes([counts, zero, jnp.broadcast_to(kept, counts.shape), zero], comps)
    return moments, ext


def moment_kernel(at_comp, *refs):
    *refs, out_ref, lse_ref = refs
    moments, ext = moment_body(at_comp, refs, lse_ref)
    out_ref[:, : moments.shape[1]] = moments
    out_ref[:, moments.shape[1] :] = ext


def moment_kernel_send(at_comp, *refs):
    *refs, true_ref, up_ref, down_ref, own_ref, lse_ref = refs
    pay_ref = refs[0]
    moments, ext = moment_body(at_comp, refs, lse_ref)
    half, feats = up_ref.shape[0], moments.shape[1]
    ext = split_ext(ext)
    for i, ref in enumerate((up_ref, down_ref)):
        at = slice(i * half, (i + 1) * half)
        ref[:, :feats] = moments[at].astype(BF16)
        ref[:, feats:] = ext[at]
    core = lax.axis_index("c")
    place = slot(0, 0)
    values = pay_ref[:, pl.ds(place, 1), :]
    source = lax.broadcasted_iota(jnp.int32, values.shape, 0)
    true = true_ref[...]
    true = jnp.where(core == 0, true, pltpu.roll(true, 64, 1))
    lse = logsumexp(jnp.where(source == 2 * place + core, true[None], values))
    own_ref[...] = jnp.where(core == 0, lse, pltpu.roll(lse, 64, 1))


def pair_sum_kernel(mine_ref, low_ref, high_ref, own_ref, s1_ref, s2_ref, s3_ref, all_ref):
    half = low_ref.shape[0]
    quarter = own_ref.shape[0]
    for at, ref in ((slice(0, half), low_ref), (slice(half, 2 * half), high_ref)):
        all_ref[at, :] = mine_ref[at, :] + ref[...].astype(F32)
    me = lax.axis_index("zh")

    def rows(shift):
        return all_ref[pl.ds(lax.rem(me + shift, 4) * quarter, quarter), :]

    ext = all_ref[:, -EXT:]
    across = lax.broadcasted_iota(jnp.int32, ext.shape, 1)
    down = lax.broadcasted_iota(jnp.int32, ext.shape, 0)
    counts = jnp.sum(jnp.where(across == down, ext[:, 0:1] + ext[:, 1:2], 0.0), axis=0, keepdims=True)
    kept = jnp.broadcast_to(ext[0:1, 2:3] + ext[0:1, 3:4], counts.shape)
    block = jnp.zeros((quarter, EXT), F32)
    for i, row in enumerate(parts(counts, 2) + parts(kept, 2)):
        block = jnp.where(down[:quarter] == i, row, block)
    feats = all_ref.shape[1] - EXT
    own_ref[:, :feats] = rows(0)[:, :feats]
    own_ref[:, feats:] = block
    for shift, ref in ((1, s1_ref), (2, s2_ref), (3, s3_ref)):
        ref[:, :feats] = rows(shift)[:, :feats].astype(BF16)
        ref[:, feats:] = block.astype(BF16)


def finish_kernel(n_comps, own_ref, g2_ref, g1_ref, g3_ref, out_ref, log_ref, ext_ref):
    rows, cols = own_ref.shape
    feats = cols - EXT
    width = feats // 2
    me = lax.axis_index("zh")
    refs = (own_ref, g1_ref, g2_ref, g3_ref)
    for shift, ref in enumerate(refs):
        ext_ref[lax.rem(me + 4 - shift, 4)] = ref[:8, feats:].astype(F32)
    counts = sum(ext_ref[i, 0:1, :] + ext_ref[i, 1:2, :] for i in range(4))
    kept = sum(ext_ref[i, 2:3, :] + ext_ref[i, 3:4, :] for i in range(4))
    log_ref[...] = jnp.log((counts + 1.0) / (kept + float(n_comps)))
    across = lax.broadcasted_iota(jnp.int32, (rows, EXT), 1)
    down = lax.broadcasted_iota(jnp.int32, (rows, EXT), 0)
    counts = jnp.sum(jnp.where(across == down + me * rows, counts, 0.0), axis=1, keepdims=True)
    second = sum(ref[:, :width].astype(F32) for ref in refs)
    first = sum(ref[:, width:feats].astype(F32) for ref in refs)
    denom = counts + 1.0
    mean = first / denom
    out_ref[:, :width] = mean.astype(BF16)
    out_ref[:, width:] = (
        (second - 2.0 * mean * first + mean * mean * counts + 1.0) / denom
    ).astype(BF16)


def place_kernel(got_ref, mean_ref, var_ref):
    _, quarter, _ = got_ref.shape
    width = mean_ref.shape[1]
    for j in range(4):
        at = slice(j * quarter, (j + 1) * quarter)
        mean_ref[at, :] = got_ref[j, :, :width].astype(F32)
        var_ref[at, :] = got_ref[j, :, width:].astype(F32)


def ring(n, shift):
    return [(i, (i + shift) % n) for i in range(n)]


def local(embeddings, keep, means, variances, log_weights):
    own, width = embeddings.shape
    comps = means.shape[0]
    n_comps = comps * 64
    cols = 2 * width + EXT
    plane, z, core = ("x", "y"), ("zh", "zl"), "c"

    back_y = [lax.ppermute(embeddings, "y", ring(4, s)) for s in (1, 3)]
    line = [embeddings] + [lax.ppermute(embeddings, "x", ring(4, s)) for s in SHIFTS[1:]]
    line = jnp.concatenate(line, axis=0)
    pair = jnp.concatenate(back_y, axis=0)

    coef = call(coef_kernel, sds((comps, cols), BF16), 3, 4 * 2**20, 2 * 2**20)(
        means, variances, log_weights[None, :]
    )
    coef, pair = lax.optimization_barrier((coef, pair))
    coef = jnp.concatenate([coef, lax.ppermute(coef, "zl", ring(2, 1))], axis=0)
    far = lax.ppermute(line, "y", ring(4, 2))
    rest = [lax.ppermute(pair, "x", ring(4, s)) for s in SHIFTS[1:]]
    coef, far, rest = lax.optimization_barrier((coef, far, rest))

    groups = [line, jnp.concatenate([pair, rest[0]]), jnp.concatenate(rest[1:]), far]
    groups += [lax.ppermute(e, core, ring(2, 1)) for e in groups]
    n_rows = 16 * own
    flops = 2 * 2 * comps * n_rows * 2 * width
    scores, lses, feats = zip(
        *[
            call(
                score_kernel,
                (
                    sds((2 * comps, n_rows), F32),
                    sds((1, n_rows), F32),
                    sds((n_rows, 2 * width), BF16),
                ),
                5,
                flops,
            )(*es, coef)
            for es in (groups[:4], groups[4:])
        ]
    )
    flag = jnp.pad(keep.astype(F32), (0, own)).reshape(1, 2 * own)
    lse_row = sds((1, 128), F32)
    pay, true = call(pay_kernel, (sds((16, 128), F32), lse_row), 3)(flag, *lses)
    pays = lax.all_to_all(jnp.broadcast_to(pay[None], (32,) + pay.shape), plane + (core,), 0, 0)

    def moments(kernel, at, outs, *more):
        return call(
            functools.partial(kernel, at),
            outs,
            5 + len(more),
            flops,
            scratch_shapes=[pltpu.VMEM((2, 16, 128), F32)],
        )(pays, *scores, *feats, *more)

    half_sum = sds((comps // 2, cols), BF16)
    up, down, own_lse = moments(moment_kernel_send, comps, (half_sum, half_sum, lse_row), true)
    low = lax.ppermute(up, z, ring(8, 1))
    high = lax.ppermute(down, z, ring(8, 7))
    pays, up = lax.optimization_barrier((pays, up))
    mine = moments(moment_kernel, 0, sds((comps, cols), F32))
    quarter = comps // 4
    q32, q16 = sds((quarter, cols), F32), sds((quarter, cols), BF16)
    own_q, s1, s2, s3 = call(
        pair_sum_kernel,
        (q32, q16, q16, q16),
        3,
        scratch_shapes=[pltpu.VMEM((comps, cols), F32)],
    )(mine, low, high)
    g = [lax.ppermute(s, "zh", ring(4, i)) for i, s in ((2, s2), (1, s1), (3, s3))]
    result, new_log = call(
        functools.partial(finish_kernel, n_comps),
        (sds((quarter, 2 * width), BF16), sds((1, comps), F32)),
        4,
        scratch_shapes=[pltpu.VMEM((4, 8, EXT), F32)],
    )(own_q, *g)
    out = sds((comps, width), F32)
    new_means, new_vars = call(place_kernel, (out, out), 1)(lax.all_gather(result, "zh"))

    wide = embeddings.astype(F32)
    own_norm = 0.5 * jnp.sum(wide * wide, axis=1) + 0.5 * width * math.log(2.0 * math.pi)
    return new_means, new_vars, new_log.reshape(-1), own_lse[0, :own] + own_norm


def solution(mesh):
    axes = ("x", "y", "zl", "c")
    fine = Mesh(mesh.devices.reshape(4, 4, 4, 2, 2), ("zh",) + axes)
    both = ("zh",) + axes
    return jax.shard_map(
        local,
        mesh=fine,
        in_specs=(P(both, None), P(both), P(axes, None), P(axes, None), P(axes)),
        out_specs=(P(axes, None), P(axes, None), P(axes), P(both)),
        check_vma=False,
    )
```

```python
import functools
import math

import jax
import jax.numpy as jnp
from jax import lax
from jax.experimental import pallas as pl
from jax.experimental.pallas import tpu as pltpu
from jax.sharding import Mesh, PartitionSpec as P

F32 = jnp.float32
BF16 = jnp.bfloat16
EXT = 128
VMEM = pl.BlockSpec(memory_space=pltpu.VMEM)
NT = (((1,), (1,)), ((), ()))
SHIFTS = (0, 2, 1, 3)
SLOTS = (
    tuple((s, 0) for s in SHIFTS),
    ((0, 1), (0, 3), (2, 1), (2, 3)),
    ((1, 1), (1, 3), (3, 1), (3, 3)),
    tuple((s, 2) for s in SHIFTS),
)
DROPPED = 1e30
INTERPRET = False


def call(kernel, out_shape, n_in, flops=0, nbytes=0, **kw):
    many = isinstance(out_shape, (list, tuple))
    n_out = len(out_shape) if many else 1
    specs = dict(
        in_specs=[VMEM] * n_in,
        out_specs=[VMEM] * n_out if many else VMEM,
    )
    specs.update(kw)
    return pl.pallas_call(
        kernel,
        out_shape=out_shape,
        compiler_params=pltpu.CompilerParams(vmem_limit_bytes=16 * 2**20),
        cost_estimate=pl.CostEstimate(flops=flops, bytes_accessed=nbytes, transcendentals=0),
        interpret=INTERPRET,
        **specs,
    )


def sds(shape, dtype):
    return jax.ShapeDtypeStruct(shape, dtype)


def parts(col, n):
    out = []
    for _ in range(n):
        top = col.astype(BF16).astype(F32)
        out.append(top)
        col = col - top
    return out


def lanes(cols, rows):
    lane = lax.broadcasted_iota(jnp.int32, (rows, EXT), 1)
    ext = jnp.zeros((rows, EXT), F32)
    for i, col in enumerate(cols):
        ext = jnp.where(lane == i, col, ext)
    return ext


def split_ext(ext):
    counts = ext[:, 0:1] + ext[:, 1:2]
    kept = ext[:, 2:3] + ext[:, 3:4]
    return lanes(parts(counts, 2) + parts(kept, 2), ext.shape[0]).astype(BF16)


def coef_kernel(a_ref, b_ref, offset_ref, out_ref):
    rows, width = a_ref.shape
    out_ref[:, :width] = a_ref[...]
    out_ref[:, width : 2 * width] = b_ref[...]
    down = lax.broadcasted_iota(jnp.int32, (rows, rows), 0)
    across = lax.broadcasted_iota(jnp.int32, (rows, rows), 1)
    offset = jnp.sum(jnp.where(down == across, offset_ref[...], 0.0), axis=1, keepdims=True)
    out_ref[:, 2 * width :] = lanes(parts(offset, 3), rows).astype(BF16)


def square(rows):
    return rows * rows


def slot(group, k):
    back_x, back_y = SLOTS[group][k]
    x, y = lax.axis_index("x"), lax.axis_index("y")
    return lax.rem(x + 4 - back_x, 4) * 4 + lax.rem(y + 4 - back_y, 4)


def score_kernel(e0_ref, e1_ref, e2_ref, e3_ref, coef_ref, s_ref, lse_ref, feats_ref):
    rows, width = e0_ref.shape
    offset = jnp.sum(coef_ref[:, 2 * width :].astype(F32), axis=1, keepdims=True)
    for i, e_ref in enumerate((e0_ref, e1_ref, e2_ref, e3_ref)):
        at = slice(i * rows, (i + 1) * rows)
        feats_ref[at, :width] = square(e_ref[...])
        feats_ref[at, width:] = e_ref[...]
    for i in range(2):
        at = slice(i * 2 * rows, (i + 1) * 2 * rows)
        s = offset + lax.dot_general(
            coef_ref[:, : 2 * width], feats_ref[at, :], NT, preferred_element_type=F32
        )
        s_ref[:, at] = s
        top = jnp.max(s, axis=0, keepdims=True)
        lse_ref[:, at] = top + jnp.log(jnp.sum(jnp.exp(s - top), axis=0, keepdims=True))


def pay_kernel(keep_ref, own_ref, other_ref, pay_ref, true_ref):
    lane = lax.broadcasted_iota(jnp.int32, (1, 128), 1)
    first = lax.axis_index("c") == 0
    for i in range(16):
        at = slice((i // 2) * 128, (i // 2 + 1) * 128)
        own, other = own_ref[:, at], other_ref[:, at]
        if i == 0:
            true_ref[...] = own
            own = jnp.where((lane < 64) & (keep_ref[...] == 0.0), DROPPED, own)
        left, right = jnp.where(first, own, other), jnp.where(first, other, own)
        if i % 2:
            left = pltpu.roll(left, 64, 1)
        else:
            right = pltpu.roll(right, 64, 1)
        pay_ref[pl.ds(slot(i // 4, i % 4), 1), :] = jnp.where(lane < 64, left, right)


def logsumexp(x):
    top = jnp.max(x, axis=0)
    return top + jnp.log(jnp.sum(jnp.exp(x - top[None]), axis=0))


def moment_body(at_comp, refs, lse_ref):
    pay_ref, s_refs, feats_refs = refs[0], refs[1:3], refs[3:5]
    comps = 128
    lse = logsumexp(pay_ref[...])
    lse_ref[0] = lse
    lse_ref[1] = pltpu.roll(lse, 64, 1)
    lane = lax.broadcasted_iota(jnp.int32, (1, 128), 1)
    core = lax.axis_index("c")
    total = jnp.zeros((comps, 128), F32)
    moments = None
    for i, (s_ref, feats_ref) in enumerate(zip(s_refs, feats_refs, strict=True)):
        half = core if i == 0 else 1 - core
        ps = []
        for j in range(8):
            left, right = (slot(j // 2, 2 * (j % 2) + k) for k in range(2))
            there = jnp.where(
                lane < 64, lse_ref[half, pl.ds(left, 1), :], lse_ref[1 - half, pl.ds(right, 1), :]
            )
            s = s_ref[at_comp : at_comp + comps, j * 128 : (j + 1) * 128]
            p = jnp.exp(s - there).astype(BF16)
            total = total + p.astype(F32)
            ps.append(p)
        add = jnp.dot(jnp.concatenate(ps, axis=1), feats_ref[...], preferred_element_type=F32)
        moments = add if i == 0 else moments + add
    counts = jnp.sum(total, axis=1, keepdims=True)
    kept = jnp.sum(jnp.where(lse < 0.5 * DROPPED, 1.0, 0.0), axis=(0, 1), keepdims=True)
    zero = jnp.zeros_like(counts)
    ext = lanes([counts, zero, jnp.broadcast_to(kept, counts.shape), zero], comps)
    return moments, ext


def moment_kernel(at_comp, *refs):
    *refs, out_ref, lse_ref = refs
    moments, ext = moment_body(at_comp, refs, lse_ref)
    out_ref[:, : moments.shape[1]] = moments
    out_ref[:, moments.shape[1] :] = ext


def moment_kernel_send(at_comp, *refs):
    *refs, true_ref, up_ref, down_ref, own_ref, lse_ref = refs
    pay_ref = refs[0]
    moments, ext = moment_body(at_comp, refs, lse_ref)
    half, feats = up_ref.shape[0], moments.shape[1]
    ext = split_ext(ext)
    for i, ref in enumerate((up_ref, down_ref)):
        at = slice(i * half, (i + 1) * half)
        ref[:, :feats] = moments[at].astype(BF16)
        ref[:, feats:] = ext[at]
    core = lax.axis_index("c")
    place = slot(0, 0)
    values = pay_ref[:, pl.ds(place, 1), :]
    source = lax.broadcasted_iota(jnp.int32, values.shape, 0)
    true = true_ref[...]
    true = jnp.where(core == 0, true, pltpu.roll(true, 64, 1))
    lse = logsumexp(jnp.where(source == 2 * place + core, true[None], values))
    own_ref[...] = jnp.where(core == 0, lse, pltpu.roll(lse, 64, 1))


def pair_sum_kernel(mine_ref, low_ref, high_ref, own_ref, s1_ref, s2_ref, s3_ref, all_ref):
    half = low_ref.shape[0]
    quarter = own_ref.shape[0]
    for at, ref in ((slice(0, half), low_ref), (slice(half, 2 * half), high_ref)):
        all_ref[at, :] = mine_ref[at, :] + ref[...].astype(F32)
    me = lax.axis_index("zh")

    def rows(shift):
        return all_ref[pl.ds(lax.rem(me + shift, 4) * quarter, quarter), :]

    ext = all_ref[:, -EXT:]
    across = lax.broadcasted_iota(jnp.int32, ext.shape, 1)
    down = lax.broadcasted_iota(jnp.int32, ext.shape, 0)
    counts = jnp.sum(jnp.where(across == down, ext[:, 0:1] + ext[:, 1:2], 0.0), axis=0, keepdims=True)
    kept = jnp.broadcast_to(ext[0:1, 2:3] + ext[0:1, 3:4], counts.shape)
    block = jnp.zeros((quarter, EXT), F32)
    for i, row in enumerate(parts(counts, 2) + parts(kept, 2)):
        block = jnp.where(down[:quarter] == i, row, block)
    feats = all_ref.shape[1] - EXT
    own_ref[:, :feats] = rows(0)[:, :feats]
    own_ref[:, feats:] = block
    for shift, ref in ((1, s1_ref), (2, s2_ref), (3, s3_ref)):
        ref[:, :feats] = rows(shift)[:, :feats].astype(BF16)
        ref[:, feats:] = block.astype(BF16)


def finish_kernel(n_comps, own_ref, g2_ref, g1_ref, g3_ref, out_ref, log_ref, ext_ref):
    rows, cols = own_ref.shape
    feats = cols - EXT
    width = feats // 2
    me = lax.axis_index("zh")
    refs = (own_ref, g1_ref, g2_ref, g3_ref)
    for shift, ref in enumerate(refs):
        ext_ref[lax.rem(me + 4 - shift, 4)] = ref[:8, feats:].astype(F32)
    counts = sum(ext_ref[i, 0:1, :] + ext_ref[i, 1:2, :] for i in range(4))
    kept = sum(ext_ref[i, 2:3, :] + ext_ref[i, 3:4, :] for i in range(4))
    log_ref[...] = jnp.log((counts + 1.0) / (kept + float(n_comps)))
    across = lax.broadcasted_iota(jnp.int32, (rows, EXT), 1)
    down = lax.broadcasted_iota(jnp.int32, (rows, EXT), 0)
    counts = jnp.sum(jnp.where(across == down + me * rows, counts, 0.0), axis=1, keepdims=True)
    second = sum(ref[:, :width].astype(F32) for ref in refs)
    first = sum(ref[:, width:feats].astype(F32) for ref in refs)
    denom = counts + 1.0
    mean = first / denom
    out_ref[:, :width] = mean.astype(BF16)
    out_ref[:, width:] = (
        (second - 2.0 * mean * first + mean * mean * counts + 1.0) / denom
    ).astype(BF16)


def place_kernel(got_ref, mean_ref, var_ref):
    _, quarter, _ = got_ref.shape
    width = mean_ref.shape[1]
    for j in range(4):
        at = slice(j * quarter, (j + 1) * quarter)
        mean_ref[at, :] = got_ref[j, :, :width].astype(F32)
        var_ref[at, :] = got_ref[j, :, width:].astype(F32)


def ring(n, shift):
    return [(i, (i + shift) % n) for i in range(n)]


def local(embeddings, keep, means, variances, log_weights):
    own, width = embeddings.shape
    comps = means.shape[0]
    n_comps = comps * 64
    cols = 2 * width + EXT
    plane, z, core = ("x", "y"), ("zh", "zl"), "c"

    back_y = [lax.ppermute(embeddings, "y", ring(4, s)) for s in (1, 3)]
    line = [embeddings] + [lax.ppermute(embeddings, "x", ring(4, s)) for s in SHIFTS[1:]]
    pair = jnp.concatenate(back_y, axis=0)

    prec = 1.0 / variances
    offset = (
        log_weights
        - 0.5 * jnp.sum(means * means * prec + jnp.log(variances), axis=1)
        - 0.5 * width * math.log(2.0 * math.pi)
    )
    coef = call(coef_kernel, sds((comps, cols), BF16), 3, 0, 2**20)(
        (-0.5 * prec).astype(BF16), (means * prec).astype(BF16), offset[None, :]
    )
    coef, line[1] = lax.optimization_barrier((coef, line[1]))
    line = jnp.concatenate(line, axis=0)
    coef = jnp.concatenate([coef, lax.ppermute(coef, "zl", ring(2, 1))], axis=0)
    far = lax.ppermute(line, "y", ring(4, 2))
    rest = [lax.ppermute(pair, "x", ring(4, s)) for s in SHIFTS[1:]]
    coef, far, rest = lax.optimization_barrier((coef, far, rest))

    groups = [line, jnp.concatenate([pair, rest[0]]), jnp.concatenate(rest[1:]), far]
    groups += [lax.ppermute(e, core, ring(2, 1)) for e in groups]
    n_rows = 16 * own
    flops = 2 * 2 * comps * n_rows * 2 * width
    scores, lses, feats = zip(
        *[
            call(
                score_kernel,
                (
                    sds((2 * comps, n_rows), F32),
                    sds((1, n_rows), F32),
                    sds((n_rows, 2 * width), BF16),
                ),
                5,
                flops,
            )(*es, coef)
            for es in (groups[:4], groups[4:])
        ]
    )
    flag = jnp.pad(keep.astype(F32), (0, own)).reshape(1, 2 * own)
    lse_row = sds((1, 128), F32)
    pay, true = call(pay_kernel, (sds((16, 128), F32), lse_row), 3)(flag, *lses)
    pays = lax.all_to_all(jnp.broadcast_to(pay[None], (32,) + pay.shape), plane + (core,), 0, 0)

    def moments(kernel, at, outs, *more):
        return call(
            functools.partial(kernel, at),
            outs,
            5 + len(more),
            flops,
            scratch_shapes=[pltpu.VMEM((2, 16, 128), F32)],
        )(pays, *scores, *feats, *more)

    half_sum = sds((comps // 2, cols), BF16)
    up, down, own_lse = moments(moment_kernel_send, comps, (half_sum, half_sum, lse_row), true)
    low = lax.ppermute(up, z, ring(8, 1))
    high = lax.ppermute(down, z, ring(8, 7))
    pays, up = lax.optimization_barrier((pays, up))
    mine = moments(moment_kernel, 0, sds((comps, cols), F32))
    quarter = comps // 4
    q32, q16 = sds((quarter, cols), F32), sds((quarter, cols), BF16)
    own_q, s1, s2, s3 = call(
        pair_sum_kernel,
        (q32, q16, q16, q16),
        3,
        scratch_shapes=[pltpu.VMEM((comps, cols), F32)],
    )(mine, low, high)
    g = [lax.ppermute(s, "zh", ring(4, i)) for i, s in ((2, s2), (1, s1), (3, s3))]
    result, new_log = call(
        functools.partial(finish_kernel, n_comps),
        (sds((quarter, 2 * width), BF16), sds((1, comps), F32)),
        4,
        scratch_shapes=[pltpu.VMEM((4, 8, EXT), F32)],
    )(own_q, *g)
    out = sds((comps, width), F32)
    new_means, new_vars = call(place_kernel, (out, out), 1)(lax.all_gather(result, "zh"))

    wide = embeddings.astype(F32)
    own_norm = 0.5 * jnp.sum(wide * wide, axis=1) + 0.5 * width * math.log(2.0 * math.pi)
    return new_means, new_vars, new_log.reshape(-1), own_lse[0, :own] + own_norm


def solution(mesh):
    axes = ("x", "y", "zl", "c")
    fine = Mesh(mesh.devices.reshape(4, 4, 4, 2, 2), ("zh",) + axes)
    both = ("zh",) + axes
    return jax.shard_map(
        local,
        mesh=fine,
        in_specs=(P(both, None), P(both), P(axes, None), P(axes, None), P(axes)),
        out_specs=(P(axes, None), P(axes, None), P(axes), P(both)),
        check_vma=False,
    )
```

```python
import functools
import math

import jax
import jax.numpy as jnp
from jax import lax
from jax.experimental import pallas as pl
from jax.experimental.pallas import tpu as pltpu
from jax.sharding import Mesh, PartitionSpec as P

F32 = jnp.float32
BF16 = jnp.bfloat16
EXT = 128
VMEM = pl.BlockSpec(memory_space=pltpu.VMEM)
NT = (((1,), (1,)), ((), ()))
SHIFTS = (0, 2, 1, 3)
SLOTS = (
    tuple((s, 0) for s in SHIFTS),
    ((0, 1), (0, 3), (2, 1), (2, 3)),
    ((1, 1), (1, 3), (3, 1), (3, 3)),
    tuple((s, 2) for s in SHIFTS),
)
DROPPED = 1e30
INTERPRET = False


def call(kernel, out_shape, n_in, flops=0, nbytes=0, **kw):
    many = isinstance(out_shape, (list, tuple))
    n_out = len(out_shape) if many else 1
    specs = dict(
        in_specs=[VMEM] * n_in,
        out_specs=[VMEM] * n_out if many else VMEM,
    )
    specs.update(kw)
    return pl.pallas_call(
        kernel,
        out_shape=out_shape,
        compiler_params=pltpu.CompilerParams(vmem_limit_bytes=16 * 2**20),
        cost_estimate=pl.CostEstimate(flops=flops, bytes_accessed=nbytes, transcendentals=0),
        interpret=INTERPRET,
        **specs,
    )


def sds(shape, dtype):
    return jax.ShapeDtypeStruct(shape, dtype)


def parts(col, n):
    out = []
    for _ in range(n):
        top = col.astype(BF16).astype(F32)
        out.append(top)
        col = col - top
    return out


def lanes(cols, rows):
    lane = lax.broadcasted_iota(jnp.int32, (rows, EXT), 1)
    ext = jnp.zeros((rows, EXT), F32)
    for i, col in enumerate(cols):
        ext = jnp.where(lane == i, col, ext)
    return ext


def split_ext(ext):
    counts = ext[:, 0:1] + ext[:, 1:2]
    kept = ext[:, 2:3] + ext[:, 3:4]
    return lanes(parts(counts, 2) + parts(kept, 2), ext.shape[0]).astype(BF16)


def coef_kernel(a_ref, b_ref, offset_ref, out_ref):
    rows, width = a_ref.shape
    out_ref[:, :width] = a_ref[...]
    out_ref[:, width : 2 * width] = b_ref[...]
    down = lax.broadcasted_iota(jnp.int32, (rows, rows), 0)
    across = lax.broadcasted_iota(jnp.int32, (rows, rows), 1)
    offset = jnp.sum(jnp.where(down == across, offset_ref[...], 0.0), axis=1, keepdims=True)
    out_ref[:, 2 * width :] = lanes(parts(offset, 3), rows).astype(BF16)


def square(rows):
    return rows * rows


def slot(group, k):
    back_x, back_y = SLOTS[group][k]
    x, y = lax.axis_index("x"), lax.axis_index("y")
    return lax.rem(x + 4 - back_x, 4) * 4 + lax.rem(y + 4 - back_y, 4)


def score_kernel(*refs):
    *e_refs, coef_ref, s_ref, lse_ref, feats_ref = refs
    rows, width = e_refs[0].shape
    offset = jnp.sum(coef_ref[:, 2 * width :].astype(F32), axis=1, keepdims=True)
    for i, e_ref in enumerate(e_refs):
        at = slice(i * rows, (i + 1) * rows)
        feats_ref[at, :width] = square(e_ref[...])
        feats_ref[at, width:] = e_ref[...]
    for i in range(len(e_refs) // 2):
        at = slice(i * 2 * rows, (i + 1) * 2 * rows)
        s = offset + lax.dot_general(
            coef_ref[:, : 2 * width], feats_ref[at, :], NT, preferred_element_type=F32
        )
        s_ref[:, at] = s
        top = jnp.max(s, axis=0, keepdims=True)
        lse_ref[:, at] = top + jnp.log(jnp.sum(jnp.exp(s - top), axis=0, keepdims=True))


def pay_kernel(keep_ref, own_ref, other_a_ref, other_b_ref, pay_ref, true_ref):
    lane = lax.broadcasted_iota(jnp.int32, (1, 128), 1)
    first = lax.axis_index("c") == 0
    for i in range(16):
        at = slice((i // 2) * 128, (i // 2 + 1) * 128)
        own = own_ref[:, at]
        there = slice(at.start % 512, at.start % 512 + 128)
        other = (other_a_ref if i < 8 else other_b_ref)[:, there]
        if i == 0:
            true_ref[...] = own
            own = jnp.where((lane < 64) & (keep_ref[...] == 0.0), DROPPED, own)
        left, right = jnp.where(first, own, other), jnp.where(first, other, own)
        if i % 2:
            left = pltpu.roll(left, 64, 1)
        else:
            right = pltpu.roll(right, 64, 1)
        pay_ref[pl.ds(slot(i // 4, i % 4), 1), :] = jnp.where(lane < 64, left, right)


def logsumexp(x):
    top = jnp.max(x, axis=0)
    return top + jnp.log(jnp.sum(jnp.exp(x - top[None]), axis=0))


def moment_body(at_comp, refs, lse_ref):
    pay_ref, s_refs, feats_refs = refs[0], refs[1:4], refs[4:7]
    comps = 128
    lse = logsumexp(pay_ref[...])
    lse_ref[0] = lse
    lse_ref[1] = pltpu.roll(lse, 64, 1)
    lane = lax.broadcasted_iota(jnp.int32, (1, 128), 1)
    core = lax.axis_index("c")
    total = jnp.zeros((comps, 128), F32)
    moments = None
    for i, (s_ref, feats_ref) in enumerate(zip(s_refs, feats_refs, strict=True)):
        half = core if i == 0 else 1 - core
        skip = 4 if i == 2 else 0
        ps = []
        for j in range(skip, skip + s_ref.shape[1] // 128):
            left, right = (slot(j // 2, 2 * (j % 2) + k) for k in range(2))
            there = jnp.where(
                lane < 64, lse_ref[half, pl.ds(left, 1), :], lse_ref[1 - half, pl.ds(right, 1), :]
            )
            s = s_ref[at_comp : at_comp + comps, (j - skip) * 128 : (j - skip + 1) * 128]
            p = jnp.exp(s - there).astype(BF16)
            total = total + p.astype(F32)
            ps.append(p)
        add = jnp.dot(jnp.concatenate(ps, axis=1), feats_ref[...], preferred_element_type=F32)
        moments = add if i == 0 else moments + add
    counts = jnp.sum(total, axis=1, keepdims=True)
    kept = jnp.sum(jnp.where(lse < 0.5 * DROPPED, 1.0, 0.0), axis=(0, 1), keepdims=True)
    zero = jnp.zeros_like(counts)
    ext = lanes([counts, zero, jnp.broadcast_to(kept, counts.shape), zero], comps)
    return moments, ext


def moment_kernel(at_comp, *refs):
    *refs, out_ref, lse_ref = refs
    moments, ext = moment_body(at_comp, refs, lse_ref)
    out_ref[:, : moments.shape[1]] = moments
    out_ref[:, moments.shape[1] :] = ext


def moment_kernel_send(at_comp, *refs):
    *refs, true_ref, up_ref, down_ref, own_ref, lse_ref = refs
    pay_ref = refs[0]
    moments, ext = moment_body(at_comp, refs, lse_ref)
    half, feats = up_ref.shape[0], moments.shape[1]
    ext = split_ext(ext)
    for i, ref in enumerate((up_ref, down_ref)):
        at = slice(i * half, (i + 1) * half)
        ref[:, :feats] = moments[at].astype(BF16)
        ref[:, feats:] = ext[at]
    core = lax.axis_index("c")
    place = slot(0, 0)
    values = pay_ref[:, pl.ds(place, 1), :]
    source = lax.broadcasted_iota(jnp.int32, values.shape, 0)
    true = true_ref[...]
    true = jnp.where(core == 0, true, pltpu.roll(true, 64, 1))
    lse = logsumexp(jnp.where(source == 2 * place + core, true[None], values))
    own_ref[...] = jnp.where(core == 0, lse, pltpu.roll(lse, 64, 1))


def pair_sum_kernel(mine_ref, low_ref, high_ref, own_ref, s1_ref, s2_ref, s3_ref, all_ref):
    half = low_ref.shape[0]
    quarter = own_ref.shape[0]
    for at, ref in ((slice(0, half), low_ref), (slice(half, 2 * half), high_ref)):
        all_ref[at, :] = mine_ref[at, :] + ref[...].astype(F32)
    me = lax.axis_index("zh")

    def rows(shift):
        return all_ref[pl.ds(lax.rem(me + shift, 4) * quarter, quarter), :]

    ext = all_ref[:, -EXT:]
    across = lax.broadcasted_iota(jnp.int32, ext.shape, 1)
    down = lax.broadcasted_iota(jnp.int32, ext.shape, 0)
    counts = jnp.sum(jnp.where(across == down, ext[:, 0:1] + ext[:, 1:2], 0.0), axis=0, keepdims=True)
    kept = jnp.broadcast_to(ext[0:1, 2:3] + ext[0:1, 3:4], counts.shape)
    block = jnp.zeros((quarter, EXT), F32)
    for i, row in enumerate(parts(counts, 2) + parts(kept, 2)):
        block = jnp.where(down[:quarter] == i, row, block)
    feats = all_ref.shape[1] - EXT
    own_ref[:, :feats] = rows(0)[:, :feats]
    own_ref[:, feats:] = block
    for shift, ref in ((1, s1_ref), (2, s2_ref), (3, s3_ref)):
        ref[:, :feats] = rows(shift)[:, :feats].astype(BF16)
        ref[:, feats:] = block.astype(BF16)


def finish_kernel(n_comps, own_ref, g2_ref, g1_ref, g3_ref, out_ref, log_ref, ext_ref):
    rows, cols = own_ref.shape
    feats = cols - EXT
    width = feats // 2
    me = lax.axis_index("zh")
    refs = (own_ref, g1_ref, g2_ref, g3_ref)
    for shift, ref in enumerate(refs):
        ext_ref[lax.rem(me + 4 - shift, 4)] = ref[:8, feats:].astype(F32)
    counts = sum(ext_ref[i, 0:1, :] + ext_ref[i, 1:2, :] for i in range(4))
    kept = sum(ext_ref[i, 2:3, :] + ext_ref[i, 3:4, :] for i in range(4))
    log_ref[...] = jnp.log((counts + 1.0) / (kept + float(n_comps)))
    across = lax.broadcasted_iota(jnp.int32, (rows, EXT), 1)
    down = lax.broadcasted_iota(jnp.int32, (rows, EXT), 0)
    counts = jnp.sum(jnp.where(across == down + me * rows, counts, 0.0), axis=1, keepdims=True)
    second = sum(ref[:, :width].astype(F32) for ref in refs)
    first = sum(ref[:, width:feats].astype(F32) for ref in refs)
    denom = counts + 1.0
    mean = first / denom
    out_ref[:, :width] = mean.astype(BF16)
    out_ref[:, width:] = (
        (second - 2.0 * mean * first + mean * mean * counts + 1.0) / denom
    ).astype(BF16)


def place_kernel(got_ref, mean_ref, var_ref):
    _, quarter, _ = got_ref.shape
    width = mean_ref.shape[1]
    for j in range(4):
        at = slice(j * quarter, (j + 1) * quarter)
        mean_ref[at, :] = got_ref[j, :, :width].astype(F32)
        var_ref[at, :] = got_ref[j, :, width:].astype(F32)


def ring(n, shift):
    return [(i, (i + shift) % n) for i in range(n)]


def local(embeddings, keep, means, variances, log_weights):
    own, width = embeddings.shape
    comps = means.shape[0]
    n_comps = comps * 64
    cols = 2 * width + EXT
    plane, z, core = ("x", "y"), ("zh", "zl"), "c"

    back_y = [lax.ppermute(embeddings, "y", ring(4, s)) for s in (1, 3)]
    line = [embeddings] + [lax.ppermute(embeddings, "x", ring(4, s)) for s in SHIFTS[1:]]
    pair = jnp.concatenate(back_y, axis=0)

    prec = 1.0 / variances
    offset = (
        log_weights
        - 0.5 * jnp.sum(means * means * prec + jnp.log(variances), axis=1)
        - 0.5 * width * math.log(2.0 * math.pi)
    )
    coef = call(coef_kernel, sds((comps, cols), BF16), 3, 0, 2**20)(
        (-0.5 * prec).astype(BF16), (means * prec).astype(BF16), offset[None, :]
    )
    coef, line[1] = lax.optimization_barrier((coef, line[1]))
    line = jnp.concatenate(line, axis=0)
    coef = jnp.concatenate([coef, lax.ppermute(coef, "zl", ring(2, 1))], axis=0)
    far = lax.ppermute(line, "y", ring(4, 2))
    rest = [lax.ppermute(pair, "x", ring(4, s)) for s in SHIFTS[1:]]
    coef, far, rest = lax.optimization_barrier((coef, far, rest))

    groups = [line, jnp.concatenate([pair, rest[0]]), jnp.concatenate(rest[1:]), far]
    groups += [lax.ppermute(e, core, ring(2, 1)) for e in groups]
    n_rows = 16 * own
    flops = 2 * 2 * comps * n_rows * 2 * width
    scores, lses, feats = zip(
        *[
            call(
                score_kernel,
                (
                    sds((2 * comps, len(es) * 4 * own), F32),
                    sds((1, len(es) * 4 * own), F32),
                    sds((len(es) * 4 * own, 2 * width), BF16),
                ),
                len(es) + 1,
                flops * len(es) // 4,
            )(*es, coef)
            for es in (groups[:4], groups[4:6], groups[6:])
        ]
    )
    flag = jnp.pad(keep.astype(F32), (0, own)).reshape(1, 2 * own)
    lse_row = sds((1, 128), F32)
    pay, true = call(pay_kernel, (sds((16, 128), F32), lse_row), 4)(flag, *lses)
    pays = lax.all_to_all(jnp.broadcast_to(pay[None], (32,) + pay.shape), plane + (core,), 0, 0)

    def moments(kernel, at, outs, *more):
        return call(
            functools.partial(kernel, at),
            outs,
            7 + len(more),
            flops,
            scratch_shapes=[pltpu.VMEM((2, 16, 128), F32)],
        )(pays, *scores, *feats, *more)

    half_sum = sds((comps // 2, cols), BF16)
    up, down, own_lse = moments(moment_kernel_send, comps, (half_sum, half_sum, lse_row), true)
    low = lax.ppermute(up, z, ring(8, 1))
    high = lax.ppermute(down, z, ring(8, 7))
    pays, up = lax.optimization_barrier((pays, up))
    mine = moments(moment_kernel, 0, sds((comps, cols), F32))
    quarter = comps // 4
    q32, q16 = sds((quarter, cols), F32), sds((quarter, cols), BF16)
    own_q, s1, s2, s3 = call(
        pair_sum_kernel,
        (q32, q16, q16, q16),
        3,
        scratch_shapes=[pltpu.VMEM((comps, cols), F32)],
    )(mine, low, high)
    g = [lax.ppermute(s, "zh", ring(4, i)) for i, s in ((2, s2), (1, s1), (3, s3))]
    result, new_log = call(
        functools.partial(finish_kernel, n_comps),
        (sds((quarter, 2 * width), BF16), sds((1, comps), F32)),
        4,
        scratch_shapes=[pltpu.VMEM((4, 8, EXT), F32)],
    )(own_q, *g)
    out = sds((comps, width), F32)
    new_means, new_vars = call(place_kernel, (out, out), 1)(lax.all_gather(result, "zh"))

    wide = embeddings.astype(F32)
    own_norm = 0.5 * jnp.sum(wide * wide, axis=1) + 0.5 * width * math.log(2.0 * math.pi)
    return new_means, new_vars, new_log.reshape(-1), own_lse[0, :own] + own_norm


def solution(mesh):
    axes = ("x", "y", "zl", "c")
    fine = Mesh(mesh.devices.reshape(4, 4, 4, 2, 2), ("zh",) + axes)
    both = ("zh",) + axes
    return jax.shard_map(
        local,
        mesh=fine,
        in_specs=(P(both, None), P(both), P(axes, None), P(axes, None), P(axes)),
        out_specs=(P(axes, None), P(axes, None), P(axes), P(both)),
        check_vma=False,
    )
```

```python
import functools
import math

import jax
import jax.numpy as jnp
from jax import lax
from jax.experimental import pallas as pl
from jax.experimental.pallas import tpu as pltpu
from jax.sharding import Mesh, PartitionSpec as P

F32 = jnp.float32
BF16 = jnp.bfloat16
EXT = 128
VMEM = pl.BlockSpec(memory_space=pltpu.VMEM)
NT = (((1,), (1,)), ((), ()))
SHIFTS = (0, 1, 3, 2)
SLOTS = (
    tuple((s, 0) for s in SHIFTS),
    ((0, 1), (0, 3), (2, 1), (2, 3)),
    ((1, 1), (1, 3), (3, 1), (3, 3)),
    tuple((s, 2) for s in SHIFTS),
)
DROPPED = 1e30
INTERPRET = False


def call(kernel, out_shape, n_in, flops=0, nbytes=0, **kw):
    many = isinstance(out_shape, (list, tuple))
    n_out = len(out_shape) if many else 1
    specs = dict(
        in_specs=[VMEM] * n_in,
        out_specs=[VMEM] * n_out if many else VMEM,
    )
    specs.update(kw)
    return pl.pallas_call(
        kernel,
        out_shape=out_shape,
        compiler_params=pltpu.CompilerParams(vmem_limit_bytes=16 * 2**20),
        cost_estimate=pl.CostEstimate(flops=flops, bytes_accessed=nbytes, transcendentals=0),
        interpret=INTERPRET,
        **specs,
    )


def sds(shape, dtype):
    return jax.ShapeDtypeStruct(shape, dtype)


def parts(col, n):
    out = []
    for _ in range(n):
        top = col.astype(BF16).astype(F32)
        out.append(top)
        col = col - top
    return out


def lanes(cols, rows):
    lane = lax.broadcasted_iota(jnp.int32, (rows, EXT), 1)
    ext = jnp.zeros((rows, EXT), F32)
    for i, col in enumerate(cols):
        ext = jnp.where(lane == i, col, ext)
    return ext


def split_ext(ext):
    counts = ext[:, 0:1] + ext[:, 1:2]
    kept = ext[:, 2:3] + ext[:, 3:4]
    return lanes(parts(counts, 2) + parts(kept, 2), ext.shape[0]).astype(BF16)


def coef_kernel(a_ref, b_ref, offset_ref, out_ref):
    rows, width = a_ref.shape
    out_ref[:, :width] = a_ref[...]
    out_ref[:, width : 2 * width] = b_ref[...]
    down = lax.broadcasted_iota(jnp.int32, (rows, rows), 0)
    across = lax.broadcasted_iota(jnp.int32, (rows, rows), 1)
    offset = jnp.sum(jnp.where(down == across, offset_ref[...], 0.0), axis=1, keepdims=True)
    out_ref[:, 2 * width :] = lanes(parts(offset, 3), rows).astype(BF16)


def square(rows):
    return rows * rows


def slot(group, k):
    back_x, back_y = SLOTS[group][k]
    x, y = lax.axis_index("x"), lax.axis_index("y")
    return lax.rem(x + 4 - back_x, 4) * 4 + lax.rem(y + 4 - back_y, 4)


def score_kernel(*refs):
    *e_refs, coef_ref, s_ref, lse_ref, feats_ref = refs
    rows, width = e_refs[0].shape
    offset = jnp.sum(coef_ref[:, 2 * width :].astype(F32), axis=1, keepdims=True)
    for i, e_ref in enumerate(e_refs):
        at = slice(i * rows, (i + 1) * rows)
        feats_ref[at, :width] = square(e_ref[...])
        feats_ref[at, width:] = e_ref[...]
    for i in range(len(e_refs) // 2):
        at = slice(i * 2 * rows, (i + 1) * 2 * rows)
        s = offset + lax.dot_general(
            coef_ref[:, : 2 * width], feats_ref[at, :], NT, preferred_element_type=F32
        )
        s_ref[:, at] = s
        top = jnp.max(s, axis=0, keepdims=True)
        lse_ref[:, at] = top + jnp.log(jnp.sum(jnp.exp(s - top), axis=0, keepdims=True))


def pay_kernel(keep_ref, own_ref, other_a_ref, other_b_ref, pay_ref, true_ref):
    lane = lax.broadcasted_iota(jnp.int32, (1, 128), 1)
    first = lax.axis_index("c") == 0
    for i in range(16):
        at = slice((i // 2) * 128, (i // 2 + 1) * 128)
        own = own_ref[:, at]
        there = slice(at.start % 512, at.start % 512 + 128)
        other = (other_a_ref if i < 8 else other_b_ref)[:, there]
        if i == 0:
            true_ref[...] = own
            own = jnp.where((lane < 64) & (keep_ref[...] == 0.0), DROPPED, own)
        left, right = jnp.where(first, own, other), jnp.where(first, other, own)
        if i % 2:
            left = pltpu.roll(left, 64, 1)
        else:
            right = pltpu.roll(right, 64, 1)
        pay_ref[pl.ds(slot(i // 4, i % 4), 1), :] = jnp.where(lane < 64, left, right)


def logsumexp(x):
    top = jnp.max(x, axis=0)
    return top + jnp.log(jnp.sum(jnp.exp(x - top[None]), axis=0))


def moment_body(at_comp, refs, lse_ref):
    pay_ref, s_refs, feats_refs = refs[0], refs[1:4], refs[4:7]
    comps = 128
    lse = logsumexp(pay_ref[...])
    lse_ref[0] = lse
    lse_ref[1] = pltpu.roll(lse, 64, 1)
    lane = lax.broadcasted_iota(jnp.int32, (1, 128), 1)
    core = lax.axis_index("c")
    total = jnp.zeros((comps, 128), F32)
    moments = None
    for i, (s_ref, feats_ref) in enumerate(zip(s_refs, feats_refs, strict=True)):
        half = core if i == 0 else 1 - core
        skip = 4 if i == 2 else 0
        ps = []
        for j in range(skip, skip + s_ref.shape[1] // 128):
            left, right = (slot(j // 2, 2 * (j % 2) + k) for k in range(2))
            there = jnp.where(
                lane < 64, lse_ref[half, pl.ds(left, 1), :], lse_ref[1 - half, pl.ds(right, 1), :]
            )
            s = s_ref[at_comp : at_comp + comps, (j - skip) * 128 : (j - skip + 1) * 128]
            p = jnp.exp(s - there).astype(BF16)
            total = total + p.astype(F32)
            ps.append(p)
        add = jnp.dot(jnp.concatenate(ps, axis=1), feats_ref[...], preferred_element_type=F32)
        moments = add if i == 0 else moments + add
    counts = jnp.sum(total, axis=1, keepdims=True)
    kept = jnp.sum(jnp.where(lse < 0.5 * DROPPED, 1.0, 0.0), axis=(0, 1), keepdims=True)
    zero = jnp.zeros_like(counts)
    ext = lanes([counts, zero, jnp.broadcast_to(kept, counts.shape), zero], comps)
    return moments, ext


def moment_kernel(at_comp, *refs):
    *refs, out_ref, lse_ref = refs
    moments, ext = moment_body(at_comp, refs, lse_ref)
    out_ref[:, : moments.shape[1]] = moments
    out_ref[:, moments.shape[1] :] = ext


def moment_kernel_send(at_comp, *refs):
    *refs, true_ref, up_ref, down_ref, own_ref, lse_ref = refs
    pay_ref = refs[0]
    moments, ext = moment_body(at_comp, refs, lse_ref)
    half, feats = up_ref.shape[0], moments.shape[1]
    ext = split_ext(ext)
    for i, ref in enumerate((up_ref, down_ref)):
        at = slice(i * half, (i + 1) * half)
        ref[:, :feats] = moments[at].astype(BF16)
        ref[:, feats:] = ext[at]
    core = lax.axis_index("c")
    place = slot(0, 0)
    values = pay_ref[:, pl.ds(place, 1), :]
    source = lax.broadcasted_iota(jnp.int32, values.shape, 0)
    true = true_ref[...]
    true = jnp.where(core == 0, true, pltpu.roll(true, 64, 1))
    lse = logsumexp(jnp.where(source == 2 * place + core, true[None], values))
    own_ref[...] = jnp.where(core == 0, lse, pltpu.roll(lse, 64, 1))


def pair_sum_kernel(mine_ref, low_ref, high_ref, own_ref, s1_ref, s2_ref, s3_ref, all_ref):
    half = low_ref.shape[0]
    quarter = own_ref.shape[0]
    for at, ref in ((slice(0, half), low_ref), (slice(half, 2 * half), high_ref)):
        all_ref[at, :] = mine_ref[at, :] + ref[...].astype(F32)
    me = lax.axis_index("zh")

    def rows(shift):
        return all_ref[pl.ds(lax.rem(me + shift, 4) * quarter, quarter), :]

    ext = all_ref[:, -EXT:]
    across = lax.broadcasted_iota(jnp.int32, ext.shape, 1)
    down = lax.broadcasted_iota(jnp.int32, ext.shape, 0)
    counts = jnp.sum(jnp.where(across == down, ext[:, 0:1] + ext[:, 1:2], 0.0), axis=0, keepdims=True)
    kept = jnp.broadcast_to(ext[0:1, 2:3] + ext[0:1, 3:4], counts.shape)
    block = jnp.zeros((quarter, EXT), F32)
    for i, row in enumerate(parts(counts, 2) + parts(kept, 2)):
        block = jnp.where(down[:quarter] == i, row, block)
    feats = all_ref.shape[1] - EXT
    own_ref[:, :feats] = rows(0)[:, :feats]
    own_ref[:, feats:] = block
    for shift, ref in ((1, s1_ref), (2, s2_ref), (3, s3_ref)):
        ref[:, :feats] = rows(shift)[:, :feats].astype(BF16)
        ref[:, feats:] = block.astype(BF16)


def finish_kernel(n_comps, own_ref, g2_ref, g1_ref, g3_ref, out_ref, log_ref, ext_ref):
    rows, cols = own_ref.shape
    feats = cols - EXT
    width = feats // 2
    me = lax.axis_index("zh")
    refs = (own_ref, g1_ref, g2_ref, g3_ref)
    for shift, ref in enumerate(refs):
        ext_ref[lax.rem(me + 4 - shift, 4)] = ref[:16, feats:].astype(F32)
    counts = sum(ext_ref[i, 0:1, :] + ext_ref[i, 1:2, :] for i in range(4))
    kept = sum(ext_ref[i, 2:3, :] + ext_ref[i, 3:4, :] for i in range(4))
    log_ref[...] = jnp.log((counts + 1.0) / (kept + float(n_comps)))
    across = lax.broadcasted_iota(jnp.int32, (rows, EXT), 1)
    down = lax.broadcasted_iota(jnp.int32, (rows, EXT), 0)
    counts = jnp.sum(jnp.where(across == down + me * rows, counts, 0.0), axis=1, keepdims=True)
    second = sum(ref[:, :width].astype(F32) for ref in refs)
    first = sum(ref[:, width:feats].astype(F32) for ref in refs)
    denom = counts + 1.0
    mean = first / denom
    out_ref[:, :width] = mean.astype(BF16)
    out_ref[:, width:] = (
        (second - 2.0 * mean * first + mean * mean * counts + 1.0) / denom
    ).astype(BF16)


def place_kernel(got_ref, mean_ref, var_ref):
    _, quarter, _ = got_ref.shape
    width = mean_ref.shape[1]
    for j in range(4):
        at = slice(j * quarter, (j + 1) * quarter)
        mean_ref[at, :] = got_ref[j, :, :width].astype(F32)
        var_ref[at, :] = got_ref[j, :, width:].astype(F32)


def ring(n, shift):
    return [(i, (i + shift) % n) for i in range(n)]


def local(embeddings, keep, means, variances, log_weights):
    own, width = embeddings.shape
    comps = means.shape[0]
    n_comps = comps * 64
    cols = 2 * width + EXT
    plane, z, core = ("x", "y"), ("zh", "zl"), "c"

    back_y = [lax.ppermute(embeddings, "y", ring(4, s)) for s in (1, 3)]
    line = [embeddings] + [lax.ppermute(embeddings, "x", ring(4, s)) for s in SHIFTS[1:]]
    pair = jnp.concatenate(back_y, axis=0)

    prec = 1.0 / variances
    offset = (
        log_weights
        - 0.5 * jnp.sum(means * means * prec + jnp.log(variances), axis=1)
        - 0.5 * width * math.log(2.0 * math.pi)
    )
    coef = call(coef_kernel, sds((comps, cols), BF16), 3, 0, 2**20)(
        (-0.5 * prec).astype(BF16), (means * prec).astype(BF16), offset[None, :]
    )
    coef, line[1] = lax.optimization_barrier((coef, line[1]))
    line = jnp.concatenate(line, axis=0)
    coef = jnp.concatenate([coef, lax.ppermute(coef, "zl", ring(2, 1))], axis=0)
    far = lax.ppermute(line, "y", ring(4, 2))
    rest = [lax.ppermute(pair, "x", ring(4, s)) for s in (2, 1, 3)]
    coef, far, rest = lax.optimization_barrier((coef, far, rest))

    groups = [line, jnp.concatenate([pair, rest[0]]), jnp.concatenate(rest[1:]), far]
    groups += [lax.ppermute(e, core, ring(2, 1)) for e in groups]
    n_rows = 16 * own
    flops = 2 * 2 * comps * n_rows * 2 * width
    scores, lses, feats = zip(
        *[
            call(
                score_kernel,
                (
                    sds((2 * comps, len(es) * 4 * own), F32),
                    sds((1, len(es) * 4 * own), F32),
                    sds((len(es) * 4 * own, 2 * width), BF16),
                ),
                len(es) + 1,
                flops * len(es) // 4,
            )(*es, coef)
            for es in (groups[:4], groups[4:6], groups[6:])
        ]
    )
    flag = jnp.pad(keep.astype(F32), (0, own)).reshape(1, 2 * own)
    lse_row = sds((1, 128), F32)
    pay, true = call(pay_kernel, (sds((16, 128), F32), lse_row), 4)(flag, *lses)
    pays = lax.all_to_all(jnp.broadcast_to(pay[None], (32,) + pay.shape), plane + (core,), 0, 0)

    def moments(kernel, at, outs, *more):
        return call(
            functools.partial(kernel, at),
            outs,
            7 + len(more),
            flops,
            scratch_shapes=[pltpu.VMEM((2, 16, 128), F32)],
        )(pays, *scores, *feats, *more)

    half_sum = sds((comps // 2, cols), BF16)
    up, down, own_lse = moments(moment_kernel_send, comps, (half_sum, half_sum, lse_row), true)
    low = lax.ppermute(up, z, ring(8, 1))
    high = lax.ppermute(down, z, ring(8, 7))
    pays, up = lax.optimization_barrier((pays, up))
    mine = moments(moment_kernel, 0, sds((comps, cols), F32))
    quarter = comps // 4
    q32, q16 = sds((quarter, cols), F32), sds((quarter, cols), BF16)
    own_q, s1, s2, s3 = call(
        pair_sum_kernel,
        (q32, q16, q16, q16),
        3,
        scratch_shapes=[pltpu.VMEM((comps, cols), F32)],
    )(mine, low, high)
    g = [lax.ppermute(s, "zh", ring(4, i)) for i, s in ((2, s2), (1, s1), (3, s3))]
    result, new_log = call(
        functools.partial(finish_kernel, n_comps),
        (sds((quarter, 2 * width), BF16), sds((1, comps), F32)),
        4,
        scratch_shapes=[pltpu.VMEM((4, 16, EXT), F32)],
    )(own_q, *g)
    out = sds((comps, width), F32)
    new_means, new_vars = call(place_kernel, (out, out), 1)(lax.all_gather(result, "zh"))

    wide = embeddings.astype(F32)
    own_norm = 0.5 * jnp.sum(wide * wide, axis=1) + 0.5 * width * math.log(2.0 * math.pi)
    return new_means, new_vars, new_log.reshape(-1), own_lse[0, :own] + own_norm


def solution(mesh):
    axes = ("x", "y", "zl", "c")
    fine = Mesh(mesh.devices.reshape(4, 4, 4, 2, 2), ("zh",) + axes)
    both = ("zh",) + axes
    return jax.shard_map(
        local,
        mesh=fine,
        in_specs=(P(both, None), P(both), P(axes, None), P(axes, None), P(axes)),
        out_specs=(P(axes, None), P(axes, None), P(axes), P(both)),
        check_vma=False,
    )
```

```python
import functools
import math

import jax
import jax.numpy as jnp
from jax import lax
from jax.experimental import pallas as pl
from jax.experimental.pallas import tpu as pltpu
from jax.sharding import Mesh, PartitionSpec as P

F32 = jnp.float32
BF16 = jnp.bfloat16
EXT = 128
VMEM = pl.BlockSpec(memory_space=pltpu.VMEM)
NT = (((1,), (1,)), ((), ()))
SHIFTS = (0, 1, 3, 2)
SLOTS = (
    tuple((s, 0) for s in SHIFTS),
    ((0, 1), (0, 3), (2, 1), (2, 3)),
    ((1, 1), (1, 3), (3, 1), (3, 3)),
    tuple((s, 2) for s in SHIFTS),
)
DROPPED = 1e30
INTERPRET = False


def call(kernel, out_shape, n_in, flops=0, nbytes=0, **kw):
    many = isinstance(out_shape, (list, tuple))
    n_out = len(out_shape) if many else 1
    specs = dict(
        in_specs=[VMEM] * n_in,
        out_specs=[VMEM] * n_out if many else VMEM,
    )
    specs.update(kw)
    return pl.pallas_call(
        kernel,
        out_shape=out_shape,
        compiler_params=pltpu.CompilerParams(vmem_limit_bytes=16 * 2**20),
        cost_estimate=pl.CostEstimate(flops=flops, bytes_accessed=nbytes, transcendentals=0),
        interpret=INTERPRET,
        **specs,
    )


def sds(shape, dtype):
    return jax.ShapeDtypeStruct(shape, dtype)


def parts(col, n):
    out = []
    for _ in range(n):
        top = col.astype(BF16).astype(F32)
        out.append(top)
        col = col - top
    return out


def lanes(cols, rows):
    lane = lax.broadcasted_iota(jnp.int32, (rows, EXT), 1)
    ext = jnp.zeros((rows, EXT), F32)
    for i, col in enumerate(cols):
        ext = jnp.where(lane == i, col, ext)
    return ext


def split_ext(ext):
    counts = ext[:, 0:1] + ext[:, 1:2]
    kept = ext[:, 2:3] + ext[:, 3:4]
    return lanes(parts(counts, 2) + parts(kept, 2), ext.shape[0]).astype(BF16)


def coef_kernel(a_ref, b_ref, offset_ref, out_ref):
    rows, width = a_ref.shape
    out_ref[:, :width] = a_ref[...]
    out_ref[:, width : 2 * width] = b_ref[...]
    down = lax.broadcasted_iota(jnp.int32, (rows, rows), 0)
    across = lax.broadcasted_iota(jnp.int32, (rows, rows), 1)
    offset = jnp.sum(jnp.where(down == across, offset_ref[...], 0.0), axis=1, keepdims=True)
    out_ref[:, 2 * width :] = lanes(parts(offset, 3), rows).astype(BF16)


def square(rows):
    return rows * rows


def slot(group, k):
    back_x, back_y = SLOTS[group][k]
    x, y = lax.axis_index("x"), lax.axis_index("y")
    return lax.rem(x + 4 - back_x, 4) * 4 + lax.rem(y + 4 - back_y, 4)


def score_kernel(*refs):
    *e_refs, coef_ref, s_ref, lse_ref, feats_ref = refs
    rows, width = e_refs[0].shape
    offset = jnp.sum(coef_ref[:, 2 * width :].astype(F32), axis=1, keepdims=True)
    for i, e_ref in enumerate(e_refs):
        at = slice(i * rows, (i + 1) * rows)
        feats_ref[at, :width] = square(e_ref[...])
        feats_ref[at, width:] = e_ref[...]
    for i in range(len(e_refs) // 2):
        at = slice(i * 2 * rows, (i + 1) * 2 * rows)
        s = offset + lax.dot_general(
            coef_ref[:, : 2 * width], feats_ref[at, :], NT, preferred_element_type=F32
        )
        s_ref[:, at] = s
        top = jnp.max(s, axis=0, keepdims=True)
        lse_ref[:, at] = top + jnp.log(jnp.sum(jnp.exp(s - top), axis=0, keepdims=True))


def pay_kernel(keep_ref, own_ref, other_a_ref, other_b_ref, pay_ref, true_ref):
    lane = lax.broadcasted_iota(jnp.int32, (1, 128), 1)
    first = lax.axis_index("c") == 0
    for i in range(16):
        at = slice((i // 2) * 128, (i // 2 + 1) * 128)
        own = own_ref[:, at]
        there = slice(at.start % 512, at.start % 512 + 128)
        other = (other_a_ref if i < 8 else other_b_ref)[:, there]
        if i == 0:
            true_ref[...] = own
            own = jnp.where((lane < 64) & (keep_ref[...] == 0.0), DROPPED, own)
        left, right = jnp.where(first, own, other), jnp.where(first, other, own)
        if i % 2:
            left = pltpu.roll(left, 64, 1)
        else:
            right = pltpu.roll(right, 64, 1)
        pay_ref[pl.ds(slot(i // 4, i % 4), 1), :] = jnp.where(lane < 64, left, right)


def logsumexp(x):
    top = jnp.max(x, axis=0)
    return top + jnp.log(jnp.sum(jnp.exp(x - top[None]), axis=0))


def moment_body(at_comp, refs, lse_ref):
    pay_ref, s_refs, feats_refs = refs[0], refs[1:4], refs[4:7]
    comps = 128
    lse = logsumexp(pay_ref[...])
    lse_ref[0] = lse
    lse_ref[1] = pltpu.roll(lse, 64, 1)
    lane = lax.broadcasted_iota(jnp.int32, (1, 128), 1)
    core = lax.axis_index("c")
    total = jnp.zeros((comps, 128), F32)
    moments = None
    for i, (s_ref, feats_ref) in enumerate(zip(s_refs, feats_refs, strict=True)):
        half = core if i == 0 else 1 - core
        skip = 4 if i == 2 else 0
        ps = []
        for j in range(skip, skip + s_ref.shape[1] // 128):
            left, right = (slot(j // 2, 2 * (j % 2) + k) for k in range(2))
            there = jnp.where(
                lane < 64, lse_ref[half, pl.ds(left, 1), :], lse_ref[1 - half, pl.ds(right, 1), :]
            )
            s = s_ref[at_comp : at_comp + comps, (j - skip) * 128 : (j - skip + 1) * 128]
            p = jnp.exp(s - there).astype(BF16)
            total = total + p.astype(F32)
            ps.append(p)
        add = jnp.dot(jnp.concatenate(ps, axis=1), feats_ref[...], preferred_element_type=F32)
        moments = add if i == 0 else moments + add
    counts = jnp.sum(total, axis=1, keepdims=True)
    kept = jnp.sum(jnp.where(lse < 0.5 * DROPPED, 1.0, 0.0), axis=(0, 1), keepdims=True)
    zero = jnp.zeros_like(counts)
    ext = lanes([counts, zero, jnp.broadcast_to(kept, counts.shape), zero], comps)
    return moments, ext


def moment_kernel(at_comp, *refs):
    *refs, out_ref, lse_ref = refs
    moments, ext = moment_body(at_comp, refs, lse_ref)
    out_ref[:, : moments.shape[1]] = moments
    out_ref[:, moments.shape[1] :] = ext


def moment_kernel_send(at_comp, *refs):
    *refs, true_ref, up_ref, down_ref, own_ref, lse_ref = refs
    pay_ref = refs[0]
    moments, ext = moment_body(at_comp, refs, lse_ref)
    half, feats = up_ref.shape[0], moments.shape[1]
    ext = split_ext(ext)
    for i, ref in enumerate((up_ref, down_ref)):
        at = slice(i * half, (i + 1) * half)
        ref[:, :feats] = moments[at].astype(BF16)
        ref[:, feats:] = ext[at]
    core = lax.axis_index("c")
    place = slot(0, 0)
    values = pay_ref[:, pl.ds(place, 1), :]
    source = lax.broadcasted_iota(jnp.int32, values.shape, 0)
    true = true_ref[...]
    true = jnp.where(core == 0, true, pltpu.roll(true, 64, 1))
    lse = logsumexp(jnp.where(source == 2 * place + core, true[None], values))
    own_ref[...] = jnp.where(core == 0, lse, pltpu.roll(lse, 64, 1))


def pair_sum_kernel(mine_ref, low_ref, high_ref, own_ref, s1_ref, s2_ref, s3_ref, all_ref):
    half = low_ref.shape[0]
    quarter = own_ref.shape[0]
    for at, ref in ((slice(0, half), low_ref), (slice(half, 2 * half), high_ref)):
        all_ref[at, :] = mine_ref[at, :] + ref[...].astype(F32)
    me = lax.axis_index("zh")

    def rows(shift):
        return all_ref[pl.ds(lax.rem(me + shift, 4) * quarter, quarter), :]

    ext = all_ref[:, -EXT:]
    across = lax.broadcasted_iota(jnp.int32, ext.shape, 1)
    down = lax.broadcasted_iota(jnp.int32, ext.shape, 0)
    counts = jnp.sum(jnp.where(across == down, ext[:, 0:1] + ext[:, 1:2], 0.0), axis=0, keepdims=True)
    kept = jnp.broadcast_to(ext[0:1, 2:3] + ext[0:1, 3:4], counts.shape)
    block = jnp.zeros((quarter, EXT), F32)
    for i, row in enumerate(parts(counts, 2) + parts(kept, 2)):
        block = jnp.where(down[:quarter] == i, row, block)
    feats = all_ref.shape[1] - EXT
    own_ref[:, :feats] = rows(0)[:, :feats]
    own_ref[:, feats:] = block
    for shift, ref in ((1, s1_ref), (2, s2_ref), (3, s3_ref)):
        ref[:, :feats] = rows(shift)[:, :feats].astype(BF16)
        ref[:, feats:] = block.astype(BF16)


def finish_kernel(n_comps, own_ref, g2_ref, g1_ref, g3_ref, out_ref, log_ref, ext_ref):
    rows, cols = own_ref.shape
    feats = cols - EXT
    width = feats // 2
    me = lax.axis_index("zh")
    refs = (own_ref, g1_ref, g2_ref, g3_ref)
    for shift, ref in enumerate(refs):
        ext_ref[lax.rem(me + 4 - shift, 4)] = ref[:16, feats:].astype(F32)
    counts = sum(ext_ref[i, 0:1, :] + ext_ref[i, 1:2, :] for i in range(4))
    kept = sum(ext_ref[i, 2:3, :] + ext_ref[i, 3:4, :] for i in range(4))
    log_ref[...] = jnp.log((counts + 1.0) / (kept + float(n_comps)))
    across = lax.broadcasted_iota(jnp.int32, (rows, EXT), 1)
    down = lax.broadcasted_iota(jnp.int32, (rows, EXT), 0)
    counts = jnp.sum(jnp.where(across == down + me * rows, counts, 0.0), axis=1, keepdims=True)
    second = sum(ref[:, :width].astype(F32) for ref in refs)
    first = sum(ref[:, width:feats].astype(F32) for ref in refs)
    denom = counts + 1.0
    mean = first / denom
    out_ref[:, :width] = mean.astype(BF16)
    out_ref[:, width:] = (
        (second - 2.0 * mean * first + mean * mean * counts + 1.0) / denom
    ).astype(BF16)


def place_kernel(got_ref, mean_hbm, var_hbm, mean_ref, var_ref, sems):
    _, quarter, _ = got_ref.shape
    width = mean_ref.shape[1]
    copies = []
    for j in range(4):
        at = slice(j * quarter, (j + 1) * quarter)
        there = pl.ds(j * quarter, quarter)
        mean_ref[at, :] = got_ref[j, :, :width].astype(F32)
        var_ref[at, :] = got_ref[j, :, width:].astype(F32)
        for i, (ref, hbm) in enumerate(((mean_ref, mean_hbm), (var_ref, var_hbm))):
            copies.append(pltpu.make_async_copy(ref.at[there], hbm.at[there], sems.at[2 * j + i]))
            copies[-1].start()
    for copy in copies:
        copy.wait()


def ring(n, shift):
    return [(i, (i + shift) % n) for i in range(n)]


def local(embeddings, keep, means, variances, log_weights):
    own, width = embeddings.shape
    comps = means.shape[0]
    n_comps = comps * 64
    cols = 2 * width + EXT
    plane, z, core = ("x", "y"), ("zh", "zl"), "c"

    back_y = [lax.ppermute(embeddings, "y", ring(4, s)) for s in (1, 3)]
    line = [embeddings] + [lax.ppermute(embeddings, "x", ring(4, s)) for s in SHIFTS[1:]]
    pair = jnp.concatenate(back_y, axis=0)

    prec = 1.0 / variances
    offset = (
        log_weights
        - 0.5 * jnp.sum(means * means * prec + jnp.log(variances), axis=1)
        - 0.5 * width * math.log(2.0 * math.pi)
    )
    coef = call(coef_kernel, sds((comps, cols), BF16), 3, 0, 2**20)(
        (-0.5 * prec).astype(BF16), (means * prec).astype(BF16), offset[None, :]
    )
    coef, line[1] = lax.optimization_barrier((coef, line[1]))
    line = jnp.concatenate(line, axis=0)
    coef = jnp.concatenate([coef, lax.ppermute(coef, "zl", ring(2, 1))], axis=0)
    far = lax.ppermute(line, "y", ring(4, 2))
    rest = [lax.ppermute(pair, "x", ring(4, s)) for s in (2, 1, 3)]
    coef, far, rest = lax.optimization_barrier((coef, far, rest))

    groups = [line, jnp.concatenate([pair, rest[0]]), jnp.concatenate(rest[1:]), far]
    groups += [lax.ppermute(e, core, ring(2, 1)) for e in groups]
    n_rows = 16 * own
    flops = 2 * 2 * comps * n_rows * 2 * width
    scores, lses, feats = zip(
        *[
            call(
                score_kernel,
                (
                    sds((2 * comps, len(es) * 4 * own), F32),
                    sds((1, len(es) * 4 * own), F32),
                    sds((len(es) * 4 * own, 2 * width), BF16),
                ),
                len(es) + 1,
                flops * len(es) // 4,
            )(*es, coef)
            for es in (groups[:4], groups[4:6], groups[6:])
        ]
    )
    flag = jnp.pad(keep.astype(F32), (0, own)).reshape(1, 2 * own)
    lse_row = sds((1, 128), F32)
    pay, true = call(pay_kernel, (sds((16, 128), F32), lse_row), 4)(flag, *lses)
    pays = lax.all_to_all(jnp.broadcast_to(pay[None], (32,) + pay.shape), plane + (core,), 0, 0)

    def moments(kernel, at, outs, *more):
        return call(
            functools.partial(kernel, at),
            outs,
            7 + len(more),
            flops,
            scratch_shapes=[pltpu.VMEM((2, 16, 128), F32)],
        )(pays, *scores, *feats, *more)

    half_sum = sds((comps // 2, cols), BF16)
    up, down, own_lse = moments(moment_kernel_send, comps, (half_sum, half_sum, lse_row), true)
    low = lax.ppermute(up, z, ring(8, 1))
    high = lax.ppermute(down, z, ring(8, 7))
    pays, up = lax.optimization_barrier((pays, up))
    mine = moments(moment_kernel, 0, sds((comps, cols), F32))
    quarter = comps // 4
    q32, q16 = sds((quarter, cols), F32), sds((quarter, cols), BF16)
    own_q, s1, s2, s3 = call(
        pair_sum_kernel,
        (q32, q16, q16, q16),
        3,
        scratch_shapes=[pltpu.VMEM((comps, cols), F32)],
    )(mine, low, high)
    g = [lax.ppermute(s, "zh", ring(4, i)) for i, s in ((2, s2), (1, s1), (3, s3))]
    result, new_log = call(
        functools.partial(finish_kernel, n_comps),
        (sds((quarter, 2 * width), BF16), sds((1, comps), F32)),
        4,
        scratch_shapes=[pltpu.VMEM((4, 16, EXT), F32)],
    )(own_q, *g)
    out = sds((comps, width), F32)
    new_means, new_vars = call(
        place_kernel,
        (out, out),
        1,
        out_specs=[pl.BlockSpec(memory_space=pl.ANY)] * 2,
        scratch_shapes=[pltpu.VMEM((comps, width), F32)] * 2 + [pltpu.SemaphoreType.DMA((8,))],
    )(lax.all_gather(result, "zh"))

    wide = embeddings.astype(F32)
    own_norm = 0.5 * jnp.sum(wide * wide, axis=1) + 0.5 * width * math.log(2.0 * math.pi)
    return new_means, new_vars, new_log.reshape(-1), own_lse[0, :own] + own_norm


def solution(mesh):
    axes = ("x", "y", "zl", "c")
    fine = Mesh(mesh.devices.reshape(4, 4, 4, 2, 2), ("zh",) + axes)
    both = ("zh",) + axes
    return jax.shard_map(
        local,
        mesh=fine,
        in_specs=(P(both, None), P(both), P(axes, None), P(axes, None), P(axes)),
        out_specs=(P(axes, None), P(axes, None), P(axes), P(both)),
        check_vma=False,
    )
```
